768 devices in a mesh: cuts: 8 (over x, core), scan: 96 (over y, z).
Axes of the slice: x: 4, y: 8, z: 12, core: 2. Of those that a mesh axis runs over, the one named last changes fastest.
Arguments:
- object_slices: bfloat16 [8, 2, 147456], P('cuts', None, 'scan'), may hold values from -1 to 1, as said below
- probe_wave: float32 [2, 128, 128], replicated, may hold values from -6 to 6
- intensity: float32 [192, 128, 128], P('scan'), may hold values from 0.05 to 4
- positions: int32 [192, 2], P('scan'), may hold values from 0 to 256
- counts: int32 [96], P('scan'), may hold values from 1 to 2, as said below
Outputs:
- object_gradient: float32 [8, 2, 147456], P('cuts', None, 'scan')
The draws below stay inside these ranges and needn't reach their ends.
Inputs may be any that keep to these rules, and one draw needn't show every extreme that they name: `object_slices`: the entries (real, imaginary) of one cell form a complex number of modulus at most 1. The live slots of a device are its first counts[d] slots; some device has all 2 slots live.
All inputs are finite; a program needn't handle non-finite values.
Results may differ from the reference program's by a relative error of at most 0.0003.
Values may be sent and summed in bfloat16 or wider, within the bound.
A program may use at most 192 MiB of HBM per device.

```python
import math
from functools import partial
import jax
import jax.numpy as jnp
from jax import lax

WIN = 128
NO = 384
SLOTS = 2
SLICES = 8
POSITIONS = 192
N_SCAN = 96


def draw_object_slices(key, part):
    key = jax.random.fold_in(key, 1)
    amp_key, phase_key = jax.random.split(key)
    array_shape = (SLICES, NO * NO)
    modulus = jax.random.uniform(amp_key, array_shape, jnp.float32, 0.8, 1.0)
    phases = jax.random.uniform(phase_key, array_shape, jnp.float32, -math.pi, math.pi)
    return jnp.stack([modulus * jnp.cos(phases), modulus * jnp.sin(phases)], axis=1).astype(jnp.bfloat16)


def draw_counts(key, part):
    key = jax.random.fold_in(key, 2)
    base_key, full_key, pick_key = jax.random.split(key, 3)
    base_count = jax.random.randint(base_key, (N_SCAN,), 1, SLOTS // 2 + 1)
    full_slot = jax.random.randint(full_key, (N_SCAN,), 0, 4) == 0
    chosen = jax.random.randint(pick_key, (), 0, N_SCAN)
    devices = jnp.arange(N_SCAN, dtype=jnp.int32)
    return jnp.where((devices == chosen) | full_slot, SLOTS, base_count).astype(jnp.int32)


def place_ends(result, own_key, low, top_value):
    spot = [jax.random.randint(jax.random.fold_in(own_key, axis), (), 0, length) for axis, length in enumerate(result.shape)]
    widest = result.shape.index(max(result.shape))
    neighbour = spot[:widest] + [(spot[widest] + 1) % result.shape[widest]] + spot[widest + 1:]
    return result.at[tuple(spot)].set(low).at[tuple(neighbour)].set(top_value)


def steps_of(rng, dims, pieces, smallest, high):
    def one(position, shards_of):
        heights = jax.random.uniform(jax.random.fold_in(jax.random.fold_in(rng, 6), position), (shards_of,), jnp.float32, smallest / len(pieces), high / len(pieces))
        return jnp.repeat(jnp.exp(heights), dims[position] // shards_of).reshape((-1,) + (1,) * (len(dims) - position - 1))

    gain = one(*pieces[0])
    for cut in pieces[1:]:
        gain = gain * one(*cut)
    return gain


def gaussian(key, shape, width, most, kind=jnp.bfloat16):
    entries = jax.random.normal(key, shape, jnp.float32) * width
    return jnp.minimum(jnp.maximum(entries, -most), most).astype(kind)


def setup_inputs(seed: int = 0) -> dict:
    key_list = jax.random.split(jax.random.key(seed), 6)
    object_slices = draw_object_slices(jax.random.fold_in(key_list[5], 71), 0)
    probe_wave = gaussian(key_list[1], (2, WIN, WIN), 1.0, 6.0, jnp.float32)
    intensity = jnp.clip(jnp.exp(math.log(4.0) - 4.3820266 * jax.random.uniform(key_list[2], (POSITIONS, WIN, WIN), jnp.float32) ** steps_of(key_list[2], (POSITIONS, WIN, WIN), ((0, 96),), -0.2, 0.2)), 0.05, 4.0)
    positions = place_ends(jax.random.randint(key_list[3], (POSITIONS, 2), 0, NO - WIN + 1), jax.random.fold_in(key_list[3], 1), 0, NO - WIN).astype(jnp.int32)
    counts = draw_counts(jax.random.fold_in(key_list[5], 71), 0)
    return dict(object_slices=object_slices, probe_wave=probe_wave, intensity=intensity, positions=positions, counts=counts)


FRESNEL = 0.5
GRAD_SCALE = 0.25

def mat_product(left_re, left_im, right_re, right_im):
    matmul = partial(jnp.dot, precision=lax.Precision.HIGHEST, preferred_element_type=jnp.float32)
    return (matmul(left_re, right_re) - matmul(left_im, right_im), matmul(left_re, right_im) + matmul(left_im, right_re))

def dft_tables(window_size):
    index_row = jnp.arange(window_size, dtype=jnp.int32)
    products = index_row[:, None] * index_row[None, :] % window_size
    angles = -2.0 * math.pi / window_size * products.astype(jnp.float32)
    scaling = 1.0 / math.sqrt(window_size)
    four_re = jnp.cos(angles) * scaling
    four_im = jnp.sin(angles) * scaling
    frequency = jnp.where(index_row < window_size // 2, index_row, index_row - window_size).astype(jnp.float32)
    phases = -math.pi * FRESNEL / window_size * frequency * frequency
    half_re = jnp.cos(phases)
    half_im = jnp.sin(phases)
    scaled_re = half_re[:, None] * four_re - half_im[:, None] * four_im
    scaled_im = half_re[:, None] * four_im + half_im[:, None] * four_re
    kern_re, kern_im = mat_product(four_re.T, -four_im.T, scaled_re, scaled_im)
    return (four_re, four_im, kern_re, kern_im)

def sandwich(left_re, left_im, wave_re, wave_im, right_re, right_im):
    contract = partial(jnp.einsum, precision=lax.Precision.HIGHEST)
    mid_re = contract('ij,bjk->bik', left_re, wave_re) - contract('ij,bjk->bik', left_im, wave_im)
    mid_im = contract('ij,bjk->bik', left_re, wave_im) + contract('ij,bjk->bik', left_im, wave_re)
    out_re = contract('bij,jk->bik', mid_re, right_re) - contract('bij,jk->bik', mid_im, right_im)
    out_im = contract('bij,jk->bik', mid_re, right_im) + contract('bij,jk->bik', mid_im, right_re)
    return (out_re, out_im)

def complex_mul(a_re, a_im, b_re, b_im):
    return (a_re * b_re - a_im * b_im, a_re * b_im + a_im * b_re)

def conj_times(a_re, a_im, b_re, b_im):
    return (a_re * b_re + a_im * b_im, a_re * b_im - a_im * b_re)

def cut_windows(plane, corners, window_size):
    zero_index = jnp.zeros((), jnp.int32)
    return jax.vmap(lambda corner: lax.dynamic_slice(plane, (zero_index, corner[0], corner[1]), (2, window_size, window_size)))(corners)

def add_windows(plane, corners, grad_re, grad_im, window_size):
    zero_index = jnp.zeros((), jnp.int32)

    def add_one(item, accumulated):
        corner = corners[item]
        anchor = (zero_index, corner[0], corner[1])
        current = lax.dynamic_slice(accumulated, anchor, (2, window_size, window_size))
        update_piece = jnp.stack([grad_re[item], grad_im[item]])
        return lax.dynamic_update_slice(accumulated, current + update_piece, anchor)
    return lax.fori_loop(0, corners.shape[0], add_one, plane)

def residual_wave(wave_re, wave_im, measured, keep_mask, four_re, four_im):
    far_re, far_im = sandwich(four_re, four_im, wave_re, wave_im, four_re.T, four_im.T)
    excess = (far_re * far_re + far_im * far_im - measured) * keep_mask[:, None, None]
    return sandwich(four_re.T, -four_im.T, excess * far_re, excess * far_im, four_re, -four_im)

def reference(object_slices, probe_wave, intensity, positions, counts):
    four_re, four_im, kern_re, kern_im = dft_tables(WIN)
    object_field = object_slices.astype(jnp.float32).reshape(SLICES, 2, NO, NO)
    slot_index = jnp.arange(POSITIONS, dtype=jnp.int32)
    live_mask = (slot_index % SLOTS < counts[slot_index // SLOTS]).astype(jnp.float32)

    def block(gradient, inputs):
        corners, measured, keep_mask = inputs
        wave_re = jnp.broadcast_to(probe_wave[0], (SLOTS, WIN, WIN))
        wave_im = jnp.broadcast_to(probe_wave[1], (SLOTS, WIN, WIN))
        saved = []
        windows = []
        for layer in range(SLICES):
            window = cut_windows(object_field[layer], corners, WIN)
            windows.append(window)
            saved.append((wave_re, wave_im))
            trans_re, trans_im = complex_mul(wave_re, wave_im, window[:, 0], window[:, 1])
            wave_re, wave_im = sandwich(kern_re, kern_im, trans_re, trans_im, kern_re.T, kern_im.T)
        chi_re, chi_im = residual_wave(wave_re, wave_im, measured, keep_mask, four_re, four_im)
        for layer in reversed(range(SLICES)):
            back_re, back_im = sandwich(kern_re.T, -kern_im.T, chi_re, chi_im, kern_re, -kern_im)
            grad_re, grad_im = conj_times(saved[layer][0], saved[layer][1], back_re, back_im)
            gradient = gradient.at[layer].set(add_windows(gradient[layer], corners, grad_re, grad_im, WIN))
            chi_re, chi_im = conj_times(windows[layer][:, 0], windows[layer][:, 1], back_re, back_im)
        return (gradient, None)
    start_grad = jnp.zeros((SLICES, 2, NO, NO), jnp.float32)
    gradient, _ = lax.scan(block, start_grad, (positions.reshape(N_SCAN, SLOTS, 2), intensity.reshape(N_SCAN, SLOTS, WIN, WIN), live_mask.reshape(N_SCAN, SLOTS)))
    return (gradient * GRAD_SCALE).reshape(SLICES, 2, NO * NO)
```

```python
import functools

import jax
import jax.numpy as jnp
import ml_dtypes
import numpy as np
from jax import lax
from jax.experimental import pallas as pl
from jax.experimental.pallas import tpu as pltpu
from jax.sharding import PartitionSpec as P

WIN = 128
FRESNEL = 0.5
GRAD_SCALE = 0.25
NZ = 12
F32 = jnp.float32
BF16 = jnp.bfloat16
MESH = pl.DeviceIdType.MESH


def row_order():
    rho = np.arange(WIN)
    q, k, m, rr = rho // 32, (rho // 8) % 4, (rho // 4) % 2, rho % 4
    return 32 * k + 16 * (q // 2) + 8 * m + 4 * (q % 2) + rr


def split_table(mat):
    hi = mat.astype(ml_dtypes.bfloat16)
    lo = (mat - hi.astype(np.float64)).astype(ml_dtypes.bfloat16)
    return np.stack([hi, lo])


def tables():
    k = np.arange(WIN)
    four = np.exp(-2j * np.pi * ((k[:, None] * k[None, :]) % WIN) / WIN) / np.sqrt(WIN)
    freq = np.where(k < WIN // 2, k, k - WIN).astype(np.float64)
    half = np.exp(-1j * np.pi * FRESNEL * freq * freq / WIN)
    kern = np.conj(four.T) @ (half[:, None] * four)
    order = row_order()

    def right(mat):
        return split_table(np.block([[mat.real, mat.imag], [-mat.imag, mat.real]]))

    def left(mat):
        return split_table(np.block([[mat.real, -mat.imag], [mat.imag, mat.real]]))

    return np.stack(
        [
            right(kern),
            left(kern[order][:, order]),
            right(four),
            left(four[:, order]),
            left(four[order]),
        ]
    )


def dot(a, b):
    return jnp.dot(a, b, preferred_element_type=F32)


def split(x):
    hi = x.astype(BF16)
    return hi, (x - hi.astype(F32)).astype(BF16)


def sandwich(x, right, left):
    hi, lo = split(x)
    both = dot(jnp.concatenate([hi, lo], 0), right[0])
    mid = both[:WIN] + both[WIN:] + dot(hi, right[1])
    mid = jnp.concatenate([mid[:, :WIN], mid[:, WIN:]], 0)
    hi, lo = split(mid)
    both = dot(left[0], jnp.concatenate([hi, lo], 1))
    out = both[:, :WIN] + both[:, WIN:] + dot(left[1], hi)
    return jnp.concatenate([out[:WIN], out[WIN:]], 1)


def complex_mul(x, w):
    x_re, x_im, w_re, w_im = x[:, :WIN], x[:, WIN:], w[:, :WIN], w[:, WIN:]
    return jnp.concatenate([x_re * w_re - x_im * w_im, x_re * w_im + x_im * w_re], 1)


def rolled_probe(probe_ref, row_at, col_at):
    shape = (WIN, WIN)
    rho = lax.broadcasted_iota(jnp.int32, shape, 0)
    lane = lax.broadcasted_iota(jnp.int32, shape, 1)
    t = (
        32 * ((rho >> 3) & 3)
        + 16 * ((rho >> 6) & 1)
        + 8 * ((rho >> 2) & 1)
        + 4 * ((rho >> 5) & 1)
        + (rho & 3)
    )
    rows = (((t - lane - row_at) & (WIN - 1)) == 0).astype(F32).astype(BF16)
    cols = (((lane - rho - col_at) & (WIN - 1)) == 0).astype(F32).astype(BF16)
    halves = []
    for plane in range(2):
        rest = probe_ref[plane]
        total = jnp.zeros(shape, F32)
        for _ in range(3):
            part = rest.astype(BF16)
            rest = rest - part.astype(F32)
            total = total + dot(dot(rows, part).astype(BF16), cols)
        halves.append(total)
    return jnp.concatenate(halves, 1)


def swap_halves(x):
    return jnp.concatenate([x[..., 4:8, :], x[..., 0:4, :]], -2)


def kernel(
    obj_ref, aux_ref, probe_ref, inten_ref, tab_ref,
    out_ref,
    cells, cells_f32, aux_all, pieces, win, psis, wave, esend, erecv, fsend, frecv,
    a_send, a_recv, p_send, p_recv, b_send, b_recv, c_send, c_recv, e_send, e_recv, f_send, f_recv, local_sem,
):
    cut = lax.axis_index("cuts")
    me = lax.axis_index("scan")
    x, core = cut // 2, cut % 2
    y, z = me // NZ, me % NZ
    bit_a = z % 2
    bit_b = (y + z // 4) % 2
    q = 2 * bit_b + bit_a
    my_slot = (me // 32) * 8 + ((me // 8) % 4) * 2 + (me // 2) % 2

    def owner(slot):
        return (slot // 8) * 32 + ((slot // 2) % 4) * 8 + 4 * bit_b + 2 * (slot % 2) + bit_a

    def mate(dq):
        y_to = y + 1 - 2 * (y % 2) if dq >= 2 else y
        z_to = z + 1 - 2 * (z % 2) if dq % 2 else z
        return y_to * NZ + z_to

    def mate_class(dq):
        b_to = 1 - bit_b if dq >= 2 else bit_b
        a_to = 1 - bit_a if dq % 2 else bit_a
        return 2 * b_to + a_to

    def core_of(dj):
        return 1 - core if dj else core

    def cut_of(dj):
        return 2 * x + core_of(dj)

    barrier = pltpu.get_barrier_semaphore()

    def greet(d, carry):
        to = owner(lax.rem(my_slot + d, 24))
        pl.semaphore_signal(barrier, inc=1, device_id={"cuts": cut, "scan": to}, device_id_type=MESH)
        return carry

    lax.fori_loop(1, 24, greet, 0)
    for dj in range(2):
        for dq in range(4):
            if dj or dq:
                pl.semaphore_signal(
                    barrier, inc=1, device_id={"cuts": cut_of(dj), "scan": mate(dq)}, device_id_type=MESH
                )
    for d in range(1, 4):
        to = 2 * lax.rem(x + d, 4) + core
        pl.semaphore_signal(barrier, inc=1, device_id={"cuts": to, "scan": me}, device_id_type=MESH)
    pl.semaphore_wait(barrier, 33)

    def aux_copy(dq):
        return pltpu.make_async_remote_copy(
            src_ref=aux_ref, dst_ref=aux_all.at[q], send_sem=p_send.at[dq], recv_sem=p_recv.at[dq],
            device_id={"cuts": cut, "scan": mate(dq)}, device_id_type=MESH,
        )

    def cell_copy(d):
        return pltpu.make_async_remote_copy(
            src_ref=obj_ref, dst_ref=cells.at[my_slot], send_sem=a_send.at[d], recv_sem=a_recv.at[d],
            device_id={"cuts": cut, "scan": owner(lax.rem(my_slot + d, 24))}, device_id_type=MESH,
        )

    for dq in range(1, 4):
        aux_copy(dq).start()

    def start_cells(d, carry):
        cell_copy(d).start()
        return carry

    lax.fori_loop(1, 24, start_cells, 0)
    aux_all[q] = aux_ref[...]
    cells[my_slot] = obj_ref[...]

    row_at = aux_ref[pl.ds(2 * core, 1), :].astype(jnp.int32)
    col_at = aux_ref[pl.ds(2 * core + 1, 1), :].astype(jnp.int32)
    wave[...] = rolled_probe(probe_ref, row_at, col_at)

    for dq in range(1, 4):
        aux_copy(dq).wait()

    def wait_cells(d, carry):
        cell_copy(d).wait()
        return carry

    lax.fori_loop(1, 24, wait_cells, 0)
    cells_f32[...] = cells[...].astype(F32)

    tile = (8, WIN)
    sub = lax.broadcasted_iota(jnp.int32, tile, 0)
    lane = lax.broadcasted_iota(jnp.int32, tile, 1)
    low = sub < 4

    def pick(n, carry):
        qt, j = n // 2, n % 2
        a = aux_all[qt, pl.ds(2 * j, 1), :].astype(jnp.int32)
        b = aux_all[qt, pl.ds(2 * j + 1, 1), :].astype(jnp.int32)
        row0 = (sub & 3) + (16 * bit_b + 4 * bit_a) - a
        in_c0 = ((lane - b) & -WIN) == 0
        in_c1 = ((lane + WIN - b) & -WIN) == 0
        for k in range(4):
            halves = []
            for m in range(2):
                cand = []
                for third in range(3):
                    blk = third * 8 + k * 2 + m
                    c0, c1, c2 = (cells_f32[blk, 8 * c : 8 * c + 8, :] for c in range(3))
                    cand.append(jnp.where(in_c0, c0, jnp.where(in_c1, c1, c2)))
                row = row0 + (32 * k + 8 * m)
                in_r0 = (row & -WIN) == 0
                in_r1 = ((row + WIN) & -WIN) == 0
                halves.append(jnp.where(in_r0, cand[0], jnp.where(in_r1, cand[1], cand[2])))
            t0, t1 = halves
            re = jnp.where(low, t0, swap_halves(t1))
            im = jnp.where(low, swap_halves(t0), t1)
            picked[qt, j, 8 * k : 8 * k + 8, :] = re
            picked[qt, j, 32 + 8 * k : 40 + 8 * k, :] = im
        pieces[qt, j] = picked[qt, j].astype(BF16)
        return carry

    picked = esend
    lax.fori_loop(0, 8, pick, 0)

    def piece_copy(dq, dj):
        return pltpu.make_async_remote_copy(
            src_ref=pieces.at[mate_class(dq), core_of(dj)], dst_ref=win.at[cut, q],
            send_sem=b_send.at[2 * dq + dj], recv_sem=b_recv.at[2 * dq + dj],
            device_id={"cuts": cut_of(dj), "scan": mate(dq)}, device_id_type=MESH,
        )

    for dj in range(2):
        for dq in range(4):
            if dj or dq:
                piece_copy(dq, dj).start()
    win[cut, q] = pieces[q, core]
    for dj in range(2):
        for dq in range(4):
            if dj or dq:
                piece_copy(dq, dj).wait()

    def win_copy(d, k):
        return pltpu.make_async_remote_copy(
            src_ref=win.at[2 * x + k], dst_ref=win.at[2 * x + k],
            send_sem=c_send.at[2 * (d - 1) + k], recv_sem=c_recv.at[2 * (d - 1) + k],
            device_id={"cuts": 2 * lax.rem(x + d, 4) + core, "scan": me}, device_id_type=MESH,
        )

    def win_arrival(s, src_x, k):
        d = lax.rem(x - src_x + 4, 4)
        return pltpu.make_async_remote_copy(
            src_ref=win.at[s], dst_ref=win.at[s],
            send_sem=c_send.at[2 * (d - 1) + k], recv_sem=c_recv.at[2 * (d - 1) + k],
            device_id={"cuts": 2 * src_x + core, "scan": me}, device_id_type=MESH,
        )

    for k in range(2):
        for d in (1, 3, 2):
            win_copy(d, k).start()

    def window(s):
        re = jnp.concatenate([win[s, i, 0:32, :] for i in range(4)], 0)
        im = jnp.concatenate([win[s, i, 32:64, :] for i in range(4)], 0)
        return jnp.concatenate([re, im], 1).astype(F32)

    def pair(i):
        return (tab_ref[i, 0], tab_ref[i, 1])

    def forward(s, carry):
        @pl.when(s // 2 != x)
        def _():
            win_arrival(s, s // 2, s % 2).wait_recv()

        psi = wave[...]
        psis[s] = psi
        wave[...] = complex_mul(psi, window(s))

        @pl.when(s < 7)
        def _():
            wave[...] = sandwich(wave[...], pair(0), pair(1))

        return carry

    lax.fori_loop(0, 8, forward, 0)

    far = sandwich(wave[...], pair(2), pair(3))
    far_re, far_im = far[:, :WIN], far[:, WIN:]
    live = aux_ref[pl.ds(4 + core, 1), :]
    excess = (far_re * far_re + far_im * far_im - inten_ref[core]) * live
    wave[...] = sandwich(jnp.concatenate([excess * far_re, -(excess * far_im)], 1), pair(2), pair(4))

    def grad_copy(k, dq, dj):
        return pltpu.make_async_remote_copy(
            src_ref=esend.at[mate_class(dq), k], dst_ref=erecv.at[q, core],
            send_sem=e_send.at[2 * dq + dj], recv_sem=e_recv.at[2 * dq + dj],
            device_id={"cuts": cut_of(dj), "scan": mate(dq)}, device_id_type=MESH,
        )

    def backward(n, carry):
        s = 7 - n
        u = wave[...]

        @pl.when(s // 2 == x)
        def _():
            g = complex_mul(psis[s], u)
            for i in range(4):
                esend[i, s % 2, 0:32, :] = g[32 * i : 32 * i + 32, :WIN]
                esend[i, s % 2, 32:64, :] = -g[32 * i : 32 * i + 32, WIN:]

            @pl.when(s % 2 == core)
            def _():
                for dq in range(1, 4):
                    grad_copy(s % 2, dq, 0).start()

            @pl.when(s % 2 != core)
            def _():
                for dq in range(4):
                    grad_copy(s % 2, dq, 1).start()

        @pl.when(s > 2 * x)
        def _():
            wave[...] = sandwich(complex_mul(u, window(s)), pair(0), pair(1))

        return carry

    lax.fori_loop(0, 8 - 2 * x, backward, 0)
    erecv[q, core] = esend[q, core]
    for dj in range(2):
        for dq in range(4):
            if dj or dq:
                grad_copy(core_of(dj), dq, dj).wait()

    def place(k, carry):
        sums = [[[jnp.zeros(tile, F32) for _ in range(3)] for _ in range(3)] for _ in range(2)]
        for qs in range(4):
            for j in range(2):
                a = aux_all[qs, 2 * j : 2 * j + 1, :].astype(jnp.int32)
                b = aux_all[qs, 2 * j + 1 : 2 * j + 2, :].astype(jnp.int32)
                row = (sub & 3) + 8 * (sub >> 2) + (16 * bit_b + 4 * bit_a + 32 * k) - a
                in_c = [((lane + WIN * c - b) & -WIN) == 0 for c in range(3)]
                for plane in range(2):
                    val = erecv[qs, j, pl.ds(pl.multiple_of(32 * plane + 8 * k, 8), 8), :]
                    for third in range(3):
                        kept = jnp.where(((row + WIN * third) & -WIN) == 0, val, 0.0)
                        for c in range(3):
                            sums[plane][third][c] += jnp.where(in_c[c], kept, 0.0)
        for third in range(3):
            for c in range(3):
                re, im = sums[0][third][c], sums[1][third][c]
                fsend[third * 8 + 2 * k, 8 * c : 8 * c + 8, :] = jnp.where(low, re, swap_halves(im))
                fsend[third * 8 + 2 * k + 1, 8 * c : 8 * c + 8, :] = jnp.where(low, swap_halves(re), im)
        return carry

    lax.fori_loop(0, 4, place, 0)

    def sum_copy(d):
        to = lax.rem(my_slot + d, 24)
        return pltpu.make_async_remote_copy(
            src_ref=fsend.at[to], dst_ref=frecv.at[my_slot], send_sem=f_send.at[d], recv_sem=f_recv.at[d],
            device_id={"cuts": cut, "scan": owner(to)}, device_id_type=MESH,
        )

    def start_sums(d, carry):
        sum_copy(d).start()
        return carry

    lax.fori_loop(1, 24, start_sums, 0)
    frecv[my_slot] = fsend[my_slot]

    for k in range(2):
        for d in (1, 3, 2):
            win_copy(d, k).wait_send()

    def wait_sums(d, carry):
        sum_copy(d).wait()
        return carry

    lax.fori_loop(1, 24, wait_sums, 0)
    total = frecv[0]
    for i in range(1, 24):
        total = total + frecv[i]
    out_ref[...] = total * GRAD_SCALE


def body(tab, object_slices, probe_wave, intensity, positions, counts):
    slots = jnp.arange(2, dtype=jnp.int32)
    live = (slots < counts[0]).astype(F32)
    rows = jnp.concatenate([positions.astype(F32).reshape(4), live, jnp.zeros((2,), F32)])
    aux = jnp.broadcast_to(rows[:, None], (8, WIN))
    obj = object_slices.reshape(2, 4, 3, WIN).transpose(2, 0, 1, 3).reshape(24, WIN)
    vmem = pl.BlockSpec(memory_space=pltpu.VMEM)
    dma = pltpu.SemaphoreType.DMA
    out = pl.pallas_call(
        kernel,
        out_shape=jax.ShapeDtypeStruct((24, WIN), F32),
        in_specs=[vmem] * 5,
        out_specs=vmem,
        scratch_shapes=[
            pltpu.VMEM((24, 24, WIN), BF16),
            pltpu.VMEM((24, 24, WIN), F32),
            pltpu.VMEM((4, 8, WIN), F32),
            pltpu.VMEM((4, 2, 64, WIN), BF16),
            pltpu.VMEM((8, 4, 64, WIN), BF16),
            pltpu.VMEM((8, WIN, 2 * WIN), F32),
            pltpu.VMEM((WIN, 2 * WIN), F32),
            pltpu.VMEM((4, 2, 64, WIN), F32),
            pltpu.VMEM((4, 2, 64, WIN), F32),
            pltpu.VMEM((24, 24, WIN), F32),
            pltpu.VMEM((24, 24, WIN), F32),
            dma((24,)), dma((24,)), dma((4,)), dma((4,)), dma((8,)), dma((8,)),
            dma((6,)), dma((6,)), dma((8,)), dma((8,)), dma((24,)), dma((24,)), dma((1,)),
        ],
        compiler_params=pltpu.CompilerParams(
            collective_id=0, has_side_effects=True, vmem_limit_bytes=32 << 20
        ),
    )(obj, aux, probe_wave, intensity, tab)
    return out.reshape(3, 2, 4, WIN).transpose(1, 2, 0, 3).reshape(1, 2, 12 * WIN)


def solution(mesh):
    tab = tables()
    in_specs = (P("cuts", None, "scan"), P(), P("scan", None, None), P("scan", None), P("scan"))
    out_specs = P("cuts", None, "scan")
    return jax.shard_map(
        functools.partial(body, tab), mesh=mesh, in_specs=in_specs, out_specs=out_specs, check_vma=False
    )
```

```python
import functools

import jax
import jax.numpy as jnp
import ml_dtypes
import numpy as np
from jax import lax
from jax.experimental import pallas as pl
from jax.experimental.pallas import tpu as pltpu
from jax.sharding import PartitionSpec as P

WIN = 128
FRESNEL = 0.5
GRAD_SCALE = 0.25
NZ = 12
F32 = jnp.float32
BF16 = jnp.bfloat16
MESH = pl.DeviceIdType.MESH


def row_order():
    rho = np.arange(WIN)
    q, h, k, rr = rho // 16, (rho // 8) % 2, (rho // 4) % 2, rho % 4
    return 64 * h + 32 * k + 16 * (q // 4) + 4 * (q % 4) + rr


def split_table(mat):
    hi = mat.astype(ml_dtypes.bfloat16)
    lo = (mat - hi.astype(np.float64)).astype(ml_dtypes.bfloat16)
    return np.stack([hi, lo])


def tables():
    k = np.arange(WIN)
    four = np.exp(-2j * np.pi * ((k[:, None] * k[None, :]) % WIN) / WIN) / np.sqrt(WIN)
    freq = np.where(k < WIN // 2, k, k - WIN).astype(np.float64)
    half = np.exp(-1j * np.pi * FRESNEL * freq * freq / WIN)
    kern = np.conj(four.T) @ (half[:, None] * four)
    order = row_order()

    def right(mat):
        return split_table(np.block([[mat.real, mat.imag], [-mat.imag, mat.real]]))

    def left(mat):
        return split_table(np.block([[mat.real, -mat.imag], [mat.imag, mat.real]]))

    return np.stack(
        [
            right(kern),
            left(kern[order][:, order]),
            right(four),
            left(four[:, order]),
            left(four[order]),
        ]
    )


def dot(a, b):
    return jnp.dot(a, b, preferred_element_type=F32)


def split(x):
    hi = x.astype(BF16)
    return hi, (x - hi.astype(F32)).astype(BF16)


def sandwich(x, right, left):
    hi, lo = split(x)
    both = dot(jnp.concatenate([hi, lo], 0), right[0])
    mid = both[:WIN] + both[WIN:] + dot(hi, right[1])
    mid = jnp.concatenate([mid[:, :WIN], mid[:, WIN:]], 0)
    hi, lo = split(mid)
    both = dot(left[0], jnp.concatenate([hi, lo], 1))
    out = both[:, :WIN] + both[:, WIN:] + dot(left[1], hi)
    return jnp.concatenate([out[:WIN], out[WIN:]], 1)


def complex_mul(x, w):
    x_re, x_im, w_re, w_im = x[:, :WIN], x[:, WIN:], w[:, :WIN], w[:, WIN:]
    return jnp.concatenate([x_re * w_re - x_im * w_im, x_re * w_im + x_im * w_re], 1)


def rolled_probe(probe_ref, row_at, col_at):
    shape = (WIN, WIN)
    rho = lax.broadcasted_iota(jnp.int32, shape, 0)
    lane = lax.broadcasted_iota(jnp.int32, shape, 1)
    t = (
        64 * ((rho >> 3) & 1)
        + 32 * ((rho >> 2) & 1)
        + 16 * ((rho >> 6) & 1)
        + 4 * ((rho >> 4) & 3)
        + (rho & 3)
    )
    rows = (((t - lane - row_at) & (WIN - 1)) == 0).astype(F32).astype(BF16)
    cols = (((lane - rho - col_at) & (WIN - 1)) == 0).astype(F32).astype(BF16)
    halves = []
    for plane in range(2):
        rest = probe_ref[plane]
        total = jnp.zeros(shape, F32)
        for _ in range(3):
            part = rest.astype(BF16)
            rest = rest - part.astype(F32)
            total = total + dot(dot(rows, part).astype(BF16), cols)
        halves.append(total)
    return jnp.concatenate(halves, 1)


def swap_halves(x):
    return jnp.concatenate([x[..., 4:8, :], x[..., 0:4, :]], -2)


def rem(a, b):
    return lax.rem(a, jnp.int32(b))


def div(a, b):
    return lax.div(a, jnp.int32(b))


def kernel(
    obj_ref, pos_ref, counts_ref, probe_ref, inten_ref, tab_ref,
    out_ref,
    obj, pos, counts, probe, inten, tab,
    cells, strips, aux_all, pieces, win, psis, wave, esend, erecv, fsend, frecv,
    in_sems, near_sems, a_sem, p_sem, b_send, b_recv, e_send, e_recv, f_sem,
):
    cut = lax.axis_index("cuts")
    me = lax.axis_index("scan")
    x, core = div(cut, 2), rem(cut, 2)
    y, z = div(me, NZ), rem(me, NZ)
    z_block, z_in = div(z, 4), rem(z, 4)
    y_block, y_in = div(y, 2), rem(y, 2)
    bit_b = rem(y_in + z_block, 2)
    q = 4 * bit_b + z_in
    n_mine = div(me, 8)
    row_base = 16 * bit_b + 4 * z_in

    def far(d):
        n = rem(n_mine + d, 12)
        return n, 8 * n + 4 * bit_b + z_in

    def mate(dy, dz):
        yi, zi = rem(y_in + dy, 2), rem(z_in + dz, 4)
        return 4 * yi + zi, 4 * rem(yi + z_block, 2) + zi, (2 * y_block + yi) * NZ + 4 * z_block + zi

    def at(cut_to, scan_to):
        return dict(device_id={"cuts": cut_to, "scan": scan_to}, device_id_type=MESH)

    sibling = cut + 1 - 2 * core

    def chip_at(i):
        x_to = i + (x <= i).astype(jnp.int32)
        return 2 * x_to + core

    loads = [
        (obj_ref, obj), (pos_ref, pos), (counts_ref, counts), (probe_ref, probe), (inten_ref.at[core], inten), (tab_ref, tab),
    ]
    loads = [pltpu.make_async_copy(src, dst, in_sems.at[i]) for i, (src, dst) in enumerate(loads)]
    for load in loads:
        load.start()

    barrier = pltpu.get_barrier_semaphore()
    for d in range(1, 12):
        pl.semaphore_signal(barrier, inc=1, **at(cut, far(d)[1]))
    for d in range(1, 4):
        pl.semaphore_signal(barrier, inc=1, **at(cut, mate(0, d)[2]))
    pl.semaphore_signal(barrier, inc=1, **at(cut, mate(1, 0)[2]))
    pl.semaphore_signal(barrier, inc=1, **at(sibling, me))
    for i in range(3):
        pl.semaphore_signal(barrier, inc=1, **at(chip_at(i), me))
    loads[0].wait()
    pl.semaphore_wait(barrier, 19)

    for d in range(1, 12):
        pltpu.make_async_remote_copy(
            src_ref=obj, dst_ref=cells.at[n_mine], send_sem=a_sem.at[0], recv_sem=a_sem.at[1], **at(cut, far(d)[1])
        ).start()
    cells[n_mine] = obj[...]

    pl.semaphore_signal(near_sems.at[0], inc=1, **at(cut, mate(1, 0)[2]))
    loads[1].wait()
    loads[2].wait()
    here = 4 * y_in + z_in
    sub = lax.broadcasted_iota(jnp.int32, (8, WIN), 0)
    lane = lax.broadcasted_iota(jnp.int32, (8, WIN), 1)
    mine = jnp.where(
        sub == 0, pos[0, 0], jnp.where(sub == 1, pos[0, 1], jnp.where(sub == 2, pos[1, 0], pos[1, 1]))
    )
    aux_all[here] = mine
    pl.semaphore_wait(near_sems.at[0], 1)
    pl.semaphore_signal(near_sems.at[1], inc=1, **at(sibling, me))
    for d in range(1, 8):
        pltpu.make_async_remote_copy(
            src_ref=aux_all.at[here], dst_ref=aux_all.at[here],
            send_sem=p_sem.at[0], recv_sem=p_sem.at[1], **at(cut, mate(d // 4, d % 4)[2])
        ).start()
    pl.semaphore_wait(near_sems.at[1], 1)
    for i in range(3):
        pl.semaphore_signal(near_sems.at[2], inc=1, **at(chip_at(i), me))

    loads[3].wait()
    row_at = jnp.where(core == 0, pos[0, 0], pos[1, 0])
    col_at = jnp.where(core == 0, pos[0, 1], pos[1, 1])
    wave[...] = rolled_probe(probe, row_at, col_at)
    loads[5].wait()

    pltpu.make_async_copy(aux_all.at[0:7], aux_all.at[0:7], p_sem.at[1]).wait()
    pl.semaphore_wait(near_sems.at[2], 3)
    pltpu.make_async_copy(cells.at[0:11], cells.at[0:11], a_sem.at[1]).wait()

    blocks = [cells[n].astype(F32) for n in range(12)]
    for third in range(3):
        for h in range(2):
            for c in range(3):
                for plane in range(2):
                    first = 8 * c + 4 * plane
                    rows = [blocks[4 * third + 2 * h + k][first : first + 4] for k in range(2)]
                    strips[third, h, c, plane] = jnp.concatenate(rows, 0)

    low = sub < 4
    row_here = 32 * (sub >> 2) + (sub & 3) + row_base

    def masks(p, j):
        a = aux_all[p, 2 * j : 2 * j + 1, :]
        b = aux_all[p, 2 * j + 1 : 2 * j + 2, :]
        in_row = [[((row_here + (WIN * third + 64 * h) - a) & -WIN) == 0 for third in range(3)] for h in range(2)]
        in_col = [((lane + WIN * c - b) & -WIN) == 0 for c in range(3)]
        return in_row, in_col

    def pick(p):
        for j in range(2):
            in_row, in_col = masks(p, j)
            tiles = []
            for plane in range(2):
                for h in range(2):
                    cand = []
                    for third in range(3):
                        c0, c1, c2 = (strips[third, h, c, plane] for c in range(3))
                        cand.append(jnp.where(in_col[0], c0, jnp.where(in_col[1], c1, c2)))
                    tiles.append(jnp.where(in_row[h][0], cand[0], jnp.where(in_row[h][1], cand[1], cand[2])))
            pieces[2 * p + j] = jnp.concatenate(tiles, 0).astype(BF16)

    def piece_send(p, j, x_to, to):
        pltpu.make_async_remote_copy(
            src_ref=pieces.at[2 * p + j], dst_ref=win.at[cut, q],
            send_sem=b_send, recv_sem=b_recv.at[cut], **at(2 * x_to + j, to)
        ).start()

    def own_pieces(x_to):
        piece_send(here, 1 - core, x_to, me)

        @pl.when(x != x_to)
        def _():
            piece_send(here, core, x_to, me)

    pick(here)
    pltpu.make_async_copy(pieces.at[2 * here + core], win.at[cut, q], b_recv.at[cut]).start()
    own_pieces(0)

    def pick_and_send(d, carry):
        p, _, to = mate(div(d, 4), rem(d, 4))
        pick(p)
        for j in range(2):
            piece_send(p, j, 0, to)
        return carry

    lax.fori_loop(1, 8, pick_and_send, 0)
    for x_to in range(1, 4):
        own_pieces(x_to)

        def only_send(d, carry):
            p, _, to = mate(div(d, 4), rem(d, 4))
            for j in range(2):
                piece_send(p, j, x_to, to)
            return carry

        lax.fori_loop(1, 8, only_send, 0)

    def window(s):
        w = win[s].astype(F32)
        return jnp.concatenate([w[:, 0:16].reshape(WIN, WIN), w[:, 16:32].reshape(WIN, WIN)], 1)

    def pair(i):
        return (tab[i, 0], tab[i, 1])

    def forward(s, carry):
        pltpu.make_async_copy(win.at[s], win.at[s], b_recv.at[s]).wait()
        psi = wave[...]
        psis[s] = psi
        wave[...] = complex_mul(psi, window(s))

        @pl.when(s < 7)
        def _():
            wave[...] = sandwich(wave[...], pair(0), pair(1))

        return carry

    lax.fori_loop(0, 8, forward, 0)
    loads[4].wait()

    far_field = sandwich(wave[...], pair(2), pair(3))
    far_re, far_im = far_field[:, :WIN], far_field[:, WIN:]
    live = jnp.where(core < counts[0], 1.0, 0.0).astype(F32)
    excess = (far_re * far_re + far_im * far_im - inten[...]) * live
    wave[...] = sandwich(jnp.concatenate([excess * far_re, -(excess * far_im)], 1), pair(2), pair(4))

    def backward(n, carry):
        s = 7 - n
        u = wave[...]

        @pl.when(div(s, 2) == x)
        def _():
            k = rem(s, 2)
            g = complex_mul(psis[s], u)
            esend[k] = jnp.concatenate(
                [g[:, :WIN].reshape(8, 16, WIN), -g[:, WIN:].reshape(8, 16, WIN)], 1
            )

            def send(d, carry):
                _, q_to, to = mate(div(d, 4), rem(d, 4))
                pltpu.make_async_remote_copy(
                    src_ref=esend.at[k, q_to], dst_ref=erecv.at[core, here],
                    send_sem=e_send, recv_sem=e_recv.at[core], **at(s, to)
                ).start()
                return carry

            @pl.when(k != core)
            def _():
                send(0, 0)

            @pl.when(k == core)
            def _():
                pltpu.make_async_copy(esend.at[k, q], erecv.at[core, here], e_recv.at[core]).start()

            lax.fori_loop(1, 8, send, 0)

        @pl.when(s > 2 * x)
        def _():
            wave[...] = sandwich(complex_mul(u, window(s)), pair(0), pair(1))

        return carry

    lax.fori_loop(0, 8 - 2 * x, backward, 0)

    for j in range(2):
        pltpu.make_async_copy(erecv.at[j], erecv.at[j], e_recv.at[j]).wait()

    def place(p, sums):
        sums = list(sums)
        for j in range(2):
            in_row, in_col = masks(p, j)
            for plane in range(2):
                for h in range(2):
                    val = erecv[j, p, 16 * plane + 8 * h : 16 * plane + 8 * h + 8, :]
                    for third in range(3):
                        kept = jnp.where(in_row[h][third], val, 0.0)
                        for c in range(3):
                            i = ((third * 2 + h) * 3 + c) * 2 + plane
                            sums[i] = sums[i] + jnp.where(in_col[c], kept, 0.0)
        return tuple(sums)

    sums = lax.fori_loop(0, 8, place, tuple(jnp.zeros((8, WIN), F32) for _ in range(36)))
    for half in range(6):
        for c in range(3):
            re, im = sums[(half * 3 + c) * 2], sums[(half * 3 + c) * 2 + 1]
            fsend[2 * half, 8 * c : 8 * c + 8, :] = jnp.where(low, re, swap_halves(im))
            fsend[2 * half + 1, 8 * c : 8 * c + 8, :] = jnp.where(low, swap_halves(re), im)

    for d in range(1, 12):
        n_to, to = far(d)
        pltpu.make_async_remote_copy(
            src_ref=fsend.at[n_to], dst_ref=frecv.at[n_mine], send_sem=f_sem.at[0], recv_sem=f_sem.at[1], **at(cut, to)
        ).start()
    frecv[n_mine] = fsend[n_mine]

    flat = win.reshape(64, 32, WIN)
    flat_e = esend.reshape(16, 32, WIN)
    for ref, sem in (
        (cells.at[0:11], a_sem.at[0]),
        (aux_all.at[0:7], p_sem.at[0]),
        (flat.at[0:63], b_send),
        (flat_e.at[0:15], e_send),
        (fsend.at[0:11], f_sem.at[0]),
        (frecv.at[0:11], f_sem.at[1]),
    ):
        pltpu.make_async_copy(ref, ref, sem).wait()
    total = frecv[0]
    for n in range(1, 12):
        total = total + frecv[n]
    out_ref[...] = total * GRAD_SCALE


def body(tab, object_slices, probe_wave, intensity, positions, counts):
    obj = object_slices.reshape(2, 4, 3, WIN).transpose(2, 0, 1, 3).reshape(24, WIN)
    hbm = pl.BlockSpec(memory_space=pltpu.HBM)
    vmem = pl.BlockSpec(memory_space=pltpu.VMEM)
    dma = pltpu.SemaphoreType.DMA
    out = pl.pallas_call(
        kernel,
        out_shape=jax.ShapeDtypeStruct((24, WIN), F32),
        in_specs=[hbm] * 6,
        out_specs=vmem,
        scratch_shapes=[
            pltpu.VMEM((24, WIN), BF16),
            pltpu.SMEM((2, 2), jnp.int32),
            pltpu.SMEM((1,), jnp.int32),
            pltpu.VMEM((2, WIN, WIN), F32),
            pltpu.VMEM((WIN, WIN), F32),
            pltpu.VMEM((5, 2, 2 * WIN, 2 * WIN), BF16),
            pltpu.VMEM((12, 24, WIN), BF16),
            pltpu.VMEM((3, 2, 3, 2, 8, WIN), F32),
            pltpu.VMEM((8, 8, WIN), jnp.int32),
            pltpu.VMEM((16, 32, WIN), BF16),
            pltpu.VMEM((8, 8, 32, WIN), BF16),
            pltpu.VMEM((8, WIN, 2 * WIN), F32),
            pltpu.VMEM((WIN, 2 * WIN), F32),
            pltpu.VMEM((2, 8, 32, WIN), F32),
            pltpu.VMEM((2, 8, 32, WIN), F32),
            pltpu.VMEM((12, 24, WIN), F32),
            pltpu.VMEM((12, 24, WIN), F32),
            dma((6,)),
            pltpu.SemaphoreType.REGULAR((3,)),
            dma((2,)), dma((2,)),
            dma, dma((8,)),
            dma, dma((2,)),
            dma((2,)),
        ],
        compiler_params=pltpu.CompilerParams(
            collective_id=0, has_side_effects=True, vmem_limit_bytes=63 << 20
        ),
    )(obj, positions, counts, probe_wave, intensity, tab)
    return out.reshape(3, 2, 4, WIN).transpose(1, 2, 0, 3).reshape(1, 2, 12 * WIN)


def solution(mesh):
    tab = tables()
    in_specs = (P("cuts", None, "scan"), P(), P("scan", None, None), P("scan", None), P("scan"))
    out_specs = P("cuts", None, "scan")
    return jax.shard_map(
        functools.partial(body, tab), mesh=mesh, in_specs=in_specs, out_specs=out_specs, check_vma=False
    )
```

```python
import functools

import jax
import jax.numpy as jnp
import ml_dtypes
import numpy as np
from jax import lax
from jax.experimental import pallas as pl
from jax.experimental.pallas import tpu as pltpu
from jax.sharding import PartitionSpec as P

WIN = 128
FRESNEL = 0.5
GRAD_SCALE = 0.25
NZ = 12
F32 = jnp.float32
BF16 = jnp.bfloat16
MESH = pl.DeviceIdType.MESH


def row_order():
    rho = np.arange(WIN)
    q, k, rr = rho // 8, (rho // 4) % 2, rho % 4
    return 64 * k + 16 * (q // 4) + 4 * (q % 4) + rr


def split_table(mat):
    hi = mat.astype(ml_dtypes.bfloat16)
    lo = (mat - hi.astype(np.float64)).astype(ml_dtypes.bfloat16)
    return np.stack([hi, lo])


def tables():
    k = np.arange(WIN)
    four = np.exp(-2j * np.pi * ((k[:, None] * k[None, :]) % WIN) / WIN) / np.sqrt(WIN)
    freq = np.where(k < WIN // 2, k, k - WIN).astype(np.float64)
    half = np.exp(-1j * np.pi * FRESNEL * freq * freq / WIN)
    kern = np.conj(four.T) @ (half[:, None] * four)
    order = row_order()

    def right(mat):
        return split_table(np.block([[mat.real, mat.imag], [-mat.imag, mat.real]]))

    def left(mat):
        return split_table(np.block([[mat.real, -mat.imag], [mat.imag, mat.real]]))

    return np.stack(
        [
            right(kern),
            left(kern[order][:, order]),
            right(four),
            left(four[:, order]),
            left(four[order]),
        ]
    )


def dot(a, b):
    return jnp.dot(a, b, preferred_element_type=F32)


def split(x):
    hi = x.astype(BF16)
    return hi, (x - hi.astype(F32)).astype(BF16)


def sandwich(x, right, left):
    hi, lo = split(x)
    both = dot(jnp.concatenate([hi, lo], 0), right[0])
    mid = both[:WIN] + both[WIN:] + dot(hi, right[1])
    mid = jnp.concatenate([mid[:, :WIN], mid[:, WIN:]], 0)
    hi, lo = split(mid)
    both = dot(left[0], jnp.concatenate([hi, lo], 1))
    out = both[:, :WIN] + both[:, WIN:] + dot(left[1], hi)
    return jnp.concatenate([out[:WIN], out[WIN:]], 1)


def complex_mul(x, w):
    x_re, x_im, w_re, w_im = x[:, :WIN], x[:, WIN:], w[:, :WIN], w[:, WIN:]
    return jnp.concatenate([x_re * w_re - x_im * w_im, x_re * w_im + x_im * w_re], 1)


def rolled_probe(probe_ref, row_at, col_at):
    shape = (WIN, WIN)
    rho = lax.broadcasted_iota(jnp.int32, shape, 0)
    lane = lax.broadcasted_iota(jnp.int32, shape, 1)
    t = 64 * ((rho >> 2) & 1) + 16 * ((rho >> 5) & 3) + 4 * ((rho >> 3) & 3) + (rho & 3)
    rows = (((t - lane - row_at) & (WIN - 1)) == 0).astype(F32).astype(BF16)
    cols = (((lane - rho - col_at) & (WIN - 1)) == 0).astype(F32).astype(BF16)
    halves = []
    for plane in range(2):
        rest = probe_ref[plane]
        total = jnp.zeros(shape, F32)
        for _ in range(3):
            part = rest.astype(BF16)
            rest = rest - part.astype(F32)
            total = total + dot(dot(rows, part).astype(BF16), cols)
        halves.append(total)
    return jnp.concatenate(halves, 1)


def swap_halves(x):
    return jnp.concatenate([x[..., 4:8, :], x[..., 0:4, :]], -2)


STEPS = 256
TOP = 32760.0


def scale_of(steps):
    return jnp.exp(steps.astype(F32) * (np.log(2.0) / STEPS))


def pack(re, im):
    most = jnp.maximum(jnp.abs(re), jnp.abs(im)).reshape(4, 4, 8, WIN)
    most = jnp.max(jnp.max(most, axis=1), axis=1, keepdims=True)
    steps = jnp.ceil(jnp.log(jnp.maximum(most, 1e-30)) * (STEPS / np.log(2.0))).astype(jnp.int32)
    factor = (TOP * scale_of(-steps))[:, None]
    whole_re, whole_im = (
        jnp.floor(part.reshape(4, 4, 8, WIN) * factor + 0.5).astype(jnp.int32) for part in (re, im)
    )
    both = ((whole_re << 16) | (whole_im & 0xFFFF)).reshape(16, 8, WIN)
    steps = jnp.broadcast_to(steps[:, None], (4, 4, 1, WIN)).reshape(16, 1, WIN)
    return jnp.concatenate([both, steps], 1)


def rem(a, b):
    return lax.rem(a, jnp.int32(b))


def div(a, b):
    return lax.div(a, jnp.int32(b))


def kernel(
    obj_ref, pos_ref, counts_ref, probe_ref, inten_ref, tab_ref,
    out_ref,
    raw, obj, pos, counts, probe, inten, tab,
    cells, strips, aux_all, pieces, win, psis, wave, esend, erecv, fsend, frecv,
    in_sems, near_sems, a_sem, p_sem, b_send, b_recv, e_send, e_recv, f_sem,
):
    cut = lax.axis_index("cuts")
    me = lax.axis_index("scan")
    x, core = div(cut, 2), rem(cut, 2)
    y, z = div(me, NZ), rem(me, NZ)
    z_block, z_in = div(z, 4), rem(z, 4)
    y_block, y_in = div(y, 4), rem(y, 4)
    bit_b = rem(3 * y_in + z_block, 4)
    q = 4 * bit_b + z_in
    n_mine = div(me, 16)
    row_base = 16 * bit_b + 4 * z_in

    def worker(yi, zi, j):
        return rem(yi + zi + 2 * j, 4)

    working = x == worker(y_in, z_in, core)

    def far(d):
        n = rem(n_mine + d, 6)
        return n, 16 * n + 4 * bit_b + z_in

    def mate(dy, dz):
        yi, zi = rem(y_in + dy, 4), rem(z_in + dz, 4)
        return yi, zi, 4 * rem(3 * yi + z_block, 4) + zi, (4 * y_block + yi) * NZ + 4 * z_block + zi

    def at(cut_to, scan_to):
        return dict(device_id={"cuts": cut_to, "scan": scan_to}, device_id_type=MESH)

    sibling = cut + 1 - 2 * core

    def chip_at(i):
        x_to = i + (x <= i).astype(jnp.int32)
        return 2 * x_to + core

    loads = [
        (obj_ref.at[0], raw), (pos_ref, pos), (counts_ref, counts), (probe_ref, probe), (inten_ref.at[core], inten), (tab_ref, tab),
    ]
    loads = [pltpu.make_async_copy(src, dst, in_sems.at[i]) for i, (src, dst) in enumerate(loads)]
    for load in loads:
        load.start()

    barrier = pltpu.get_barrier_semaphore()
    for d in range(1, 6):
        pl.semaphore_signal(barrier, inc=1, **at(cut, far(d)[1]))
    for d in range(1, 4):
        pl.semaphore_signal(barrier, inc=1, **at(cut, mate(0, d)[3]))
        pl.semaphore_signal(barrier, inc=1, **at(cut, mate(d, 0)[3]))
    pl.semaphore_signal(barrier, inc=1, **at(sibling, me))
    for i in range(3):
        pl.semaphore_signal(barrier, inc=1, **at(chip_at(i), me))

    loads[0].wait()
    flat_obj = raw[...].astype(F32)
    rows = []
    for c in range(3):
        for plane in range(2):
            for rr in range(4):
                first = (3 * rr + c) * WIN
                rows.append(flat_obj[plane : plane + 1, first : first + WIN])
    obj[...] = jnp.concatenate(rows, 0).astype(BF16)
    pl.semaphore_wait(barrier, 15)

    for d in range(1, 4):
        pl.semaphore_signal(near_sems.at[0], inc=1, **at(cut, mate(d, 0)[3]))

    for d in range(1, 6):
        pltpu.make_async_remote_copy(
            src_ref=obj, dst_ref=cells.at[n_mine], send_sem=a_sem.at[0], recv_sem=a_sem.at[1], **at(cut, far(d)[1])
        ).start()
    cells[n_mine] = obj[...]

    loads[1].wait()
    loads[2].wait()
    here = 4 * y_in + z_in
    sub = lax.broadcasted_iota(jnp.int32, (8, WIN), 0)
    lane = lax.broadcasted_iota(jnp.int32, (8, WIN), 1)
    mine = jnp.where(
        sub == 0, pos[0, 0], jnp.where(sub == 1, pos[0, 1], jnp.where(sub == 2, pos[1, 0], pos[1, 1]))
    )
    aux_all[here] = mine[0:4]
    pl.semaphore_wait(near_sems.at[0], 3)
    pl.semaphore_signal(near_sems.at[1], inc=1, **at(sibling, me))
    for d in range(1, 16):
        pltpu.make_async_remote_copy(
            src_ref=aux_all.at[here], dst_ref=aux_all.at[here],
            send_sem=p_sem.at[0], recv_sem=p_sem.at[1], **at(cut, mate(d // 4, d % 4)[3])
        ).start()
    pl.semaphore_wait(near_sems.at[1], 1)
    for i in range(3):
        pl.semaphore_signal(near_sems.at[2], inc=1, **at(chip_at(i), me))

    loads[3].wait()
    loads[4].wait()
    loads[5].wait()

    @pl.when(working)
    def _():
        row_at = jnp.where(core == 0, pos[0, 0], pos[1, 0])
        col_at = jnp.where(core == 0, pos[0, 1], pos[1, 1])
        wave[...] = rolled_probe(probe, row_at, col_at)

    pltpu.make_async_copy(aux_all.at[0:15], aux_all.at[0:15], p_sem.at[1]).wait()
    pl.semaphore_wait(near_sems.at[2], 3)
    pltpu.make_async_copy(cells.at[0:5], cells.at[0:5], a_sem.at[1]).wait()

    blocks = [cells[n].astype(F32) for n in range(6)]
    for third in range(3):
        for c in range(3):
            for plane in range(2):
                first = 8 * c + 4 * plane
                rows = [blocks[2 * third + k][first : first + 4] for k in range(2)]
                strips[third, c, plane] = jnp.concatenate(rows, 0)

    low = sub < 4
    row_here = 64 * (sub >> 2) + (sub & 3) + row_base

    def masks(p, j):
        a = aux_all[p, 2 * j : 2 * j + 1, :]
        b = aux_all[p, 2 * j + 1 : 2 * j + 2, :]
        in_row = [((row_here + WIN * third - a) & -WIN) == 0 for third in range(3)]
        in_col = [((lane + WIN * c - b) & -WIN) == 0 for c in range(3)]
        return in_row, in_col

    def pick(p):
        for j in range(2):
            in_row, in_col = masks(p, j)
            planes = []
            for plane in range(2):
                cand = []
                for third in range(3):
                    c0, c1, c2 = (strips[third, c, plane] for c in range(3))
                    cand.append(jnp.where(in_col[0], c0, jnp.where(in_col[1], c1, c2)))
                planes.append(jnp.where(in_row[0], cand[0], jnp.where(in_row[1], cand[1], cand[2])))
            pieces[2 * p + j] = jnp.concatenate(planes, 0).astype(BF16)

    def piece_send(yi, zi, j, to):
        pltpu.make_async_remote_copy(
            src_ref=pieces.at[2 * (4 * yi + zi) + j], dst_ref=win.at[cut, q],
            send_sem=b_send, recv_sem=b_recv.at[cut], **at(2 * worker(yi, zi, j) + j, to)
        ).start()

    def pick_and_send(d, carry):
        yi, zi, _, to = mate(div(d, 4), rem(d, 4))
        pick(4 * yi + zi)
        for j in range(2):
            piece_send(yi, zi, j, to)
        return carry

    lax.fori_loop(1, 16, pick_and_send, 0)
    pick(here)
    piece_send(y_in, z_in, 1 - core, me)

    @pl.when(working)
    def _():
        pltpu.make_async_copy(pieces.at[2 * here + core], win.at[cut, q], b_recv.at[cut]).start()

    @pl.when(jnp.logical_not(working))
    def _():
        piece_send(y_in, z_in, core, me)

    def window(s):
        w = win[s].astype(F32)
        return jnp.concatenate([w[:, 0:8].reshape(WIN, WIN), w[:, 8:16].reshape(WIN, WIN)], 1)

    def pair(i):
        return (tab[i, 0], tab[i, 1])

    def forward(s, carry):
        pltpu.make_async_copy(win.at[s], win.at[s], b_recv.at[s]).wait()
        psi = wave[...]
        psis[s] = psi
        wave[...] = complex_mul(psi, window(s))

        @pl.when(s < 7)
        def _():
            wave[...] = sandwich(wave[...], pair(0), pair(1))

        return carry

    def residual():
        far_field = sandwich(wave[...], pair(2), pair(3))
        far_re, far_im = far_field[:, :WIN], far_field[:, WIN:]
        live = jnp.where(core < counts[0], 1.0, 0.0).astype(F32)
        excess = (far_re * far_re + far_im * far_im - inten[...]) * live
        wave[...] = sandwich(jnp.concatenate([excess * far_re, -(excess * far_im)], 1), pair(2), pair(4))

    def backward(n, carry):
        s = 7 - n
        u = wave[...]
        g = complex_mul(psis[s], u)
        esend[pl.ds(16 * s, 16)] = pack(g[:, :WIN].reshape(16, 8, WIN), -g[:, WIN:].reshape(16, 8, WIN))

        def send(d, carry):
            _, _, q_to, to = mate(div(d, 4), rem(d, 4))
            pltpu.make_async_remote_copy(
                src_ref=esend.at[16 * s + q_to], dst_ref=erecv.at[core, here],
                send_sem=e_send, recv_sem=e_recv, **at(s, to)
            ).start()
            return carry

        @pl.when(s != cut)
        def _():
            send(0, 0)

        @pl.when(s == cut)
        def _():
            pltpu.make_async_copy(esend.at[16 * s + q], erecv.at[core, here], e_recv).start()

        lax.fori_loop(1, 16, send, 0)

        @pl.when(s > 0)
        def _():
            wave[...] = sandwich(complex_mul(u, window(s)), pair(0), pair(1))

        return carry

    @pl.when(working)
    def _():
        lax.fori_loop(0, 8, forward, 0)
        residual()
        lax.fori_loop(0, 8, backward, 0)

    pltpu.make_async_copy(erecv, erecv, e_recv).wait()

    def place(p, sums):
        sums = list(sums)
        for j in range(2):
            in_row, in_col = masks(p, j)
            both = erecv[j, p, 0:8, :]
            scale = scale_of(erecv[j, p, 8:9, :]) * (1.0 / TOP)
            for plane in range(2):
                val = (both if plane == 0 else both << 16) >> 16
                val = val.astype(F32) * scale
                for third in range(3):
                    kept = jnp.where(in_row[third], val, 0.0)
                    for c in range(3):
                        i = (third * 3 + c) * 2 + plane
                        sums[i] = sums[i] + jnp.where(in_col[c], kept, 0.0)
        return tuple(sums)

    sums = lax.fori_loop(0, 16, place, tuple(jnp.zeros((8, WIN), F32) for _ in range(18)))
    for third in range(3):
        for c in range(3):
            re, im = sums[(third * 3 + c) * 2], sums[(third * 3 + c) * 2 + 1]
            fsend[2 * third, 8 * c : 8 * c + 8, :] = jnp.where(low, re, swap_halves(im))
            fsend[2 * third + 1, 8 * c : 8 * c + 8, :] = jnp.where(low, swap_halves(re), im)

    for d in range(1, 6):
        n_to, to = far(d)
        pltpu.make_async_remote_copy(
            src_ref=fsend.at[n_to], dst_ref=frecv.at[n_mine], send_sem=f_sem.at[0], recv_sem=f_sem.at[1], **at(cut, to)
        ).start()
    frecv[n_mine] = fsend[n_mine]

    @pl.when(working)
    def _():
        pltpu.make_async_copy(pieces.at[0:31], pieces.at[0:31], b_send).wait()
        pltpu.make_async_copy(esend.at[0:127], esend.at[0:127], e_send).wait()

    @pl.when(jnp.logical_not(working))
    def _():
        pltpu.make_async_copy(pieces, pieces, b_send).wait()

    for ref, sem in (
        (cells.at[0:5], a_sem.at[0]),
        (aux_all.at[0:15], p_sem.at[0]),
        (fsend.at[0:5], f_sem.at[0]),
        (frecv.at[0:5], f_sem.at[1]),
    ):
        pltpu.make_async_copy(ref, ref, sem).wait()
    total = frecv[0]
    for n in range(1, 6):
        total = total + frecv[n]
    total = total * GRAD_SCALE
    for rr in range(4):
        for c in range(3):
            first = (3 * rr + c) * WIN
            both = [total[8 * c + 4 * plane + rr : 8 * c + 4 * plane + rr + 1] for plane in range(2)]
            out_ref[:, first : first + WIN] = jnp.concatenate(both, 0)


def body(tab, object_slices, probe_wave, intensity, positions, counts):
    hbm = pl.BlockSpec(memory_space=pltpu.HBM)
    vmem = pl.BlockSpec(memory_space=pltpu.VMEM)
    dma = pltpu.SemaphoreType.DMA
    out = pl.pallas_call(
        kernel,
        out_shape=pltpu.VMEM((2, 12 * WIN), F32),
        in_specs=[hbm] * 6,
        out_specs=vmem,
        scratch_shapes=[
            pltpu.VMEM((2, 12 * WIN), BF16),
            pltpu.VMEM((24, WIN), BF16),
            pltpu.SMEM((2, 2), jnp.int32),
            pltpu.SMEM((1,), jnp.int32),
            pltpu.VMEM((2, WIN, WIN), F32),
            pltpu.VMEM((WIN, WIN), F32),
            pltpu.VMEM((5, 2, 2 * WIN, 2 * WIN), BF16),
            pltpu.VMEM((6, 24, WIN), BF16),
            pltpu.VMEM((3, 3, 2, 8, WIN), F32),
            pltpu.VMEM((16, 4, WIN), jnp.int32),
            pltpu.VMEM((32, 16, WIN), BF16),
            pltpu.VMEM((8, 16, 16, WIN), BF16),
            pltpu.VMEM((8, WIN, 2 * WIN), F32),
            pltpu.VMEM((WIN, 2 * WIN), F32),
            pltpu.VMEM((128, 9, WIN), jnp.int32),
            pltpu.VMEM((2, 16, 9, WIN), jnp.int32),
            pltpu.VMEM((6, 24, WIN), F32),
            pltpu.VMEM((6, 24, WIN), F32),
            dma((6,)),
            pltpu.SemaphoreType.REGULAR((3,)),
            dma((2,)), dma((2,)),
            dma, dma((8,)),
            dma, dma,
            dma((2,)),
        ],
        compiler_params=pltpu.CompilerParams(
            collective_id=0, has_side_effects=True, vmem_limit_bytes=60 << 20
        ),
    )(object_slices, positions, counts, probe_wave, intensity, tab)
    return out.reshape(1, 2, 12 * WIN)


def solution(mesh):
    tab = tables()
    in_specs = (P("cuts", None, "scan"), P(), P("scan", None, None), P("scan", None), P("scan"))
    out_specs = P("cuts", None, "scan")
    return jax.shard_map(
        functools.partial(body, tab), mesh=mesh, in_specs=in_specs, out_specs=out_specs, check_vma=False
    )
```

```python
import functools

import jax
import jax.numpy as jnp
import ml_dtypes
import numpy as np
from jax import lax
from jax.experimental import pallas as pl
from jax.experimental.pallas import tpu as pltpu
from jax.sharding import PartitionSpec as P

WIN = 128
FRESNEL = 0.5
GRAD_SCALE = 0.25
NZ = 12
F32 = jnp.float32
BF16 = jnp.bfloat16
MESH = pl.DeviceIdType.MESH


def row_order():
    rho = np.arange(WIN)
    q, h, k, rr = rho // 16, (rho // 8) % 2, (rho // 4) % 2, rho % 4
    return 64 * h + 32 * k + 16 * (q // 4) + 4 * (q % 4) + rr


def split_table(mat):
    hi = mat.astype(ml_dtypes.bfloat16)
    lo = (mat - hi.astype(np.float64)).astype(ml_dtypes.bfloat16)
    return np.stack([hi, lo])


def tables():
    k = np.arange(WIN)
    four = np.exp(-2j * np.pi * ((k[:, None] * k[None, :]) % WIN) / WIN) / np.sqrt(WIN)
    freq = np.where(k < WIN // 2, k, k - WIN).astype(np.float64)
    half = np.exp(-1j * np.pi * FRESNEL * freq * freq / WIN)
    kern = np.conj(four.T) @ (half[:, None] * four)
    order = row_order()

    def right(mat):
        return split_table(np.block([[mat.real, mat.imag], [-mat.imag, mat.real]]))

    def left(mat):
        return split_table(np.block([[mat.real, -mat.imag], [mat.imag, mat.real]]))

    return np.stack(
        [
            right(kern),
            left(kern[order][:, order]),
            right(four),
            left(four[:, order]),
            left(four[order]),
        ]
    )


def dot(a, b):
    return jnp.dot(a, b, preferred_element_type=F32)


def split(x):
    hi = x.astype(BF16)
    return hi, (x - hi.astype(F32)).astype(BF16)


def sandwich(x, right, left):
    hi, lo = split(x)
    both = dot(jnp.concatenate([hi, lo], 0), right[0])
    mid = both[:WIN] + both[WIN:] + dot(hi, right[1])
    mid = jnp.concatenate([mid[:, :WIN], mid[:, WIN:]], 0)
    hi, lo = split(mid)
    both = dot(left[0], jnp.concatenate([hi, lo], 1))
    out = both[:, :WIN] + both[:, WIN:] + dot(left[1], hi)
    return jnp.concatenate([out[:WIN], out[WIN:]], 1)


def complex_mul(x, w):
    x_re, x_im, w_re, w_im = x[:, :WIN], x[:, WIN:], w[:, :WIN], w[:, WIN:]
    return jnp.concatenate([x_re * w_re - x_im * w_im, x_re * w_im + x_im * w_re], 1)


def rolled_probe(probe_ref, row_at, col_at):
    shape = (WIN, WIN)
    rho = lax.broadcasted_iota(jnp.int32, shape, 0)
    lane = lax.broadcasted_iota(jnp.int32, shape, 1)
    t = (
        64 * ((rho >> 3) & 1)
        + 32 * ((rho >> 2) & 1)
        + 16 * ((rho >> 6) & 1)
        + 4 * ((rho >> 4) & 3)
        + (rho & 3)
    )
    rows = (((t - lane - row_at) & (WIN - 1)) == 0).astype(F32).astype(BF16)
    cols = (((lane - rho - col_at) & (WIN - 1)) == 0).astype(F32).astype(BF16)
    halves = []
    for plane in range(2):
        rest = probe_ref[plane]
        total = jnp.zeros(shape, F32)
        for _ in range(3):
            part = rest.astype(BF16)
            rest = rest - part.astype(F32)
            total = total + dot(dot(rows, part).astype(BF16), cols)
        halves.append(total)
    return jnp.concatenate(halves, 1)


STEPS = 256
TOP = 32760.0


def scale_of(steps):
    return jnp.exp(steps.astype(F32) * (np.log(2.0) / STEPS))


def pack(re, im, groups):
    def grouped(part):
        return part.reshape(groups, -1, 8, WIN)

    most = jnp.max(grouped(jnp.maximum(jnp.abs(re), jnp.abs(im))), axis=1)
    most = jnp.max(most, axis=1, keepdims=True)
    steps = jnp.ceil(jnp.log(jnp.maximum(most, 1e-30)) * (STEPS / np.log(2.0))).astype(jnp.int32)
    factor = (TOP * scale_of(-steps))[:, None]
    whole_re, whole_im = (jnp.floor(grouped(part) * factor + 0.5).astype(jnp.int32) for part in (re, im))
    return ((whole_re << 16) | (whole_im & 0xFFFF)).reshape(re.shape), steps


def unpack(both, steps, factor):
    scale = scale_of(steps) * (factor / TOP)
    return (both >> 16).astype(F32) * scale, ((both << 16) >> 16).astype(F32) * scale


def rem(a, b):
    return lax.rem(a, jnp.int32(b))


def div(a, b):
    return lax.div(a, jnp.int32(b))


def kernel(
    obj_ref, pos_ref, counts_ref, probe_ref, inten_ref, tab_ref,
    out_ref,
    raw, obj, pos, counts, probe, inten, tab,
    cells, strips, aux_all, pieces, win, psis, wave, esend, erecv, fsend, frecv,
    in_sems, near_sems, a_sem, p_sem, b_send, b_recv, e_send, e_recv, f_sem,
):
    cut = lax.axis_index("cuts")
    me = lax.axis_index("scan")
    x, core = div(cut, 2), rem(cut, 2)
    y, z = div(me, NZ), rem(me, NZ)
    z_block, z_in = div(z, 4), rem(z, 4)
    y_block, y_in = div(y, 2), rem(y, 2)
    bit_b = rem(y_in + z_block, 2)
    q = 4 * bit_b + z_in
    n_mine = div(me, 8)
    row_base = 16 * bit_b + 4 * z_in

    def worker(yi, zi, j):
        return rem(yi + zi + j, 2)

    working = x == worker(y_in, z_in, core)

    def far(d):
        n = rem(n_mine + d, 12)
        return n, 8 * n + 4 * bit_b + z_in

    def mate(dy, dz):
        yi, zi = rem(y_in + dy, 2), rem(z_in + dz, 4)
        return yi, zi, 4 * rem(yi + z_block, 2) + zi, (2 * y_block + yi) * NZ + 4 * z_block + zi

    def at(cut_to, scan_to):
        return dict(device_id={"cuts": cut_to, "scan": scan_to}, device_id_type=MESH)

    sibling = cut + 1 - 2 * core

    def chip_at(i):
        x_to = i + (x <= i).astype(jnp.int32)
        return 2 * x_to + core

    loads = [
        (obj_ref.at[0], raw), (pos_ref, pos), (counts_ref, counts), (probe_ref, probe), (inten_ref.at[core], inten), (tab_ref, tab),
    ]
    loads = [pltpu.make_async_copy(src, dst, in_sems.at[i]) for i, (src, dst) in enumerate(loads)]
    for load in loads:
        load.start()

    barrier = pltpu.get_barrier_semaphore()
    for d in range(1, 12):
        pl.semaphore_signal(barrier, inc=1, **at(cut, far(d)[1]))
    for d in range(1, 4):
        pl.semaphore_signal(barrier, inc=1, **at(cut, mate(0, d)[3]))
    pl.semaphore_signal(barrier, inc=1, **at(cut, mate(1, 0)[3]))
    pl.semaphore_signal(barrier, inc=1, **at(sibling, me))
    for i in range(3):
        pl.semaphore_signal(barrier, inc=1, **at(chip_at(i), me))

    loads[0].wait()
    flat_obj = raw[...].astype(F32)
    rows = []
    for c in range(3):
        for plane in range(2):
            for rr in range(4):
                first = (3 * rr + c) * WIN
                rows.append(flat_obj[plane : plane + 1, first : first + WIN])
    obj[...] = jnp.concatenate(rows, 0).astype(BF16)
    pl.semaphore_wait(barrier, 19)

    pl.semaphore_signal(near_sems.at[0], inc=1, **at(cut, mate(1, 0)[3]))

    for d in range(1, 12):
        pltpu.make_async_remote_copy(
            src_ref=obj, dst_ref=cells.at[n_mine], send_sem=a_sem.at[0], recv_sem=a_sem.at[1], **at(cut, far(d)[1])
        ).start()
    cells[n_mine] = obj[...]

    loads[1].wait()
    loads[2].wait()
    here = 4 * y_in + z_in
    sub = lax.broadcasted_iota(jnp.int32, (8, WIN), 0)
    lane = lax.broadcasted_iota(jnp.int32, (8, WIN), 1)
    mine = jnp.where(
        sub == 0, pos[0, 0], jnp.where(sub == 1, pos[0, 1], jnp.where(sub == 2, pos[1, 0], pos[1, 1]))
    )
    aux_all[here] = mine[0:4]
    pl.semaphore_wait(near_sems.at[0], 1)
    pl.semaphore_signal(near_sems.at[1], inc=1, **at(sibling, me))
    for d in range(1, 8):
        pltpu.make_async_remote_copy(
            src_ref=aux_all.at[here], dst_ref=aux_all.at[here],
            send_sem=p_sem.at[0], recv_sem=p_sem.at[1], **at(cut, mate(d // 4, d % 4)[3])
        ).start()
    pl.semaphore_wait(near_sems.at[1], 1)
    for i in range(3):
        pl.semaphore_signal(near_sems.at[2], inc=1, **at(chip_at(i), me))

    loads[3].wait()
    loads[4].wait()
    loads[5].wait()

    @pl.when(working)
    def _():
        row_at = jnp.where(core == 0, pos[0, 0], pos[1, 0])
        col_at = jnp.where(core == 0, pos[0, 1], pos[1, 1])
        wave[...] = rolled_probe(probe, row_at, col_at)

    pltpu.make_async_copy(aux_all.at[0:7], aux_all.at[0:7], p_sem.at[1]).wait()
    pl.semaphore_wait(near_sems.at[2], 3)
    pltpu.make_async_copy(cells.at[0:11], cells.at[0:11], a_sem.at[1]).wait()

    blocks = [cells[n].astype(F32) for n in range(12)]
    for third in range(3):
        for h in range(2):
            for c in range(3):
                for plane in range(2):
                    first = 8 * c + 4 * plane
                    rows = [blocks[4 * third + 2 * h + k][first : first + 4] for k in range(2)]
                    strips[third, h, c, plane] = jnp.concatenate(rows, 0)

    row_here = 32 * (sub >> 2) + (sub & 3) + row_base

    def masks(p, j):
        a = aux_all[p, 2 * j : 2 * j + 1, :]
        b = aux_all[p, 2 * j + 1 : 2 * j + 2, :]
        in_row = [[((row_here + (WIN * third + 64 * h) - a) & -WIN) == 0 for third in range(3)] for h in range(2)]
        in_col = [((lane + WIN * c - b) & -WIN) == 0 for c in range(3)]
        return in_row, in_col

    def pick(p):
        for j in range(2):
            in_row, in_col = masks(p, j)
            tiles = []
            for plane in range(2):
                for h in range(2):
                    cand = []
                    for third in range(3):
                        c0, c1, c2 = (strips[third, h, c, plane] for c in range(3))
                        cand.append(jnp.where(in_col[0], c0, jnp.where(in_col[1], c1, c2)))
                    tiles.append(jnp.where(in_row[h][0], cand[0], jnp.where(in_row[h][1], cand[1], cand[2])))
            pieces[2 * p + j] = jnp.concatenate(tiles, 0).astype(BF16)

    def piece_send(yi, zi, j, to):
        pltpu.make_async_remote_copy(
            src_ref=pieces.at[2 * (4 * yi + zi) + j], dst_ref=win.at[cut, q],
            send_sem=b_send, recv_sem=b_recv.at[cut], **at(2 * worker(yi, zi, j) + j, to)
        ).start()

    def pick_and_send(d, carry):
        yi, zi, _, to = mate(div(d, 4), rem(d, 4))
        pick(4 * yi + zi)
        for j in range(2):
            piece_send(yi, zi, j, to)
        return carry

    lax.fori_loop(1, 8, pick_and_send, 0)
    pick(here)
    piece_send(y_in, z_in, 1 - core, me)

    @pl.when(working)
    def _():
        pltpu.make_async_copy(pieces.at[2 * here + core], win.at[cut, q], b_recv.at[cut]).start()

    @pl.when(jnp.logical_not(working))
    def _():
        piece_send(y_in, z_in, core, me)

    def window(s):
        w = win[s].astype(F32)
        return jnp.concatenate([w[:, 0:16].reshape(WIN, WIN), w[:, 16:32].reshape(WIN, WIN)], 1)

    def pair(i):
        return (tab[i, 0], tab[i, 1])

    def forward(s, carry):
        pltpu.make_async_copy(win.at[s], win.at[s], b_recv.at[s]).wait()
        psi = wave[...]
        psis[s] = psi
        wave[...] = complex_mul(psi, window(s))

        @pl.when(s < 7)
        def _():
            wave[...] = sandwich(wave[...], pair(0), pair(1))

        return carry

    def residual():
        far_field = sandwich(wave[...], pair(2), pair(3))
        far_re, far_im = far_field[:, :WIN], far_field[:, WIN:]
        live = jnp.where(core < counts[0], 1.0, 0.0).astype(F32)
        excess = (far_re * far_re + far_im * far_im - inten[...]) * live
        wave[...] = sandwich(jnp.concatenate([excess * far_re, -(excess * far_im)], 1), pair(2), pair(4))

    def backward(n, carry):
        s = 7 - n
        u = wave[...]
        g = complex_mul(psis[s], u)
        both, steps = pack(g[:, :WIN].reshape(8, 16, WIN), -g[:, WIN:].reshape(8, 16, WIN), 4)
        steps = jnp.broadcast_to(steps[:, None], (4, 2, 1, WIN)).reshape(8, 1, WIN)
        esend[pl.ds(8 * s, 8)] = jnp.concatenate([both, steps], 1)

        def send(d, carry):
            _, _, q_to, to = mate(div(d, 4), rem(d, 4))
            pltpu.make_async_remote_copy(
                src_ref=esend.at[8 * s + q_to], dst_ref=erecv.at[core, here],
                send_sem=e_send, recv_sem=e_recv, **at(s, to)
            ).start()
            return carry

        @pl.when(s != cut)
        def _():
            send(0, 0)

        @pl.when(s == cut)
        def _():
            pltpu.make_async_copy(esend.at[8 * s + q], erecv.at[core, here], e_recv).start()

        lax.fori_loop(1, 8, send, 0)

        @pl.when(s > 0)
        def _():
            wave[...] = sandwich(complex_mul(u, window(s)), pair(0), pair(1))

        return carry

    @pl.when(working)
    def _():
        lax.fori_loop(0, 8, forward, 0)
        residual()
        lax.fori_loop(0, 8, backward, 0)

    pltpu.make_async_copy(erecv, erecv, e_recv).wait()

    def place(p, sums):
        sums = list(sums)
        for j in range(2):
            in_row, in_col = masks(p, j)
            vals = unpack(erecv[j, p, 0:16, :], erecv[j, p, 16:17, :], 1.0)
            for plane in range(2):
                for h in range(2):
                    val = vals[plane][8 * h : 8 * h + 8]
                    for third in range(3):
                        kept = jnp.where(in_row[h][third], val, 0.0)
                        for c in range(3):
                            i = ((third * 2 + h) * 3 + c) * 2 + plane
                            sums[i] = sums[i] + jnp.where(in_col[c], kept, 0.0)
        return tuple(sums)

    sums = lax.fori_loop(0, 8, place, tuple(jnp.zeros((8, WIN), F32) for _ in range(36)))
    for half in range(6):
        re, im = (jnp.stack([sums[(half * 3 + c) * 2 + plane] for c in range(3)]) for plane in range(2))
        both, steps = pack(re, im, 1)
        for k in range(2):
            rows = [both[c, 4 * k : 4 * k + 4] for c in range(3)] + [steps[0]]
            fsend[2 * half + k] = jnp.concatenate(rows, 0)

    for d in range(1, 12):
        n_to, to = far(d)
        pltpu.make_async_remote_copy(
            src_ref=fsend.at[n_to], dst_ref=frecv.at[n_mine], send_sem=f_sem.at[0], recv_sem=f_sem.at[1], **at(cut, to)
        ).start()
    frecv[n_mine] = fsend[n_mine]

    @pl.when(working)
    def _():
        pltpu.make_async_copy(pieces.at[0:15], pieces.at[0:15], b_send).wait()
        pltpu.make_async_copy(esend.at[0:63], esend.at[0:63], e_send).wait()

    @pl.when(jnp.logical_not(working))
    def _():
        pltpu.make_async_copy(pieces, pieces, b_send).wait()

    for ref, sem in (
        (cells.at[0:11], a_sem.at[0]),
        (aux_all.at[0:7], p_sem.at[0]),
        (fsend.at[0:11], f_sem.at[0]),
        (frecv.at[0:11], f_sem.at[1]),
    ):
        pltpu.make_async_copy(ref, ref, sem).wait()
    total = [jnp.zeros((12, WIN), F32)] * 2
    for n in range(12):
        part = unpack(frecv[n, 0:12, :], frecv[n, 12:13, :], GRAD_SCALE)
        total = [total[plane] + part[plane] for plane in range(2)]
    for rr in range(4):
        for c in range(3):
            first = (3 * rr + c) * WIN
            both = [total[plane][4 * c + rr : 4 * c + rr + 1] for plane in range(2)]
            out_ref[:, first : first + WIN] = jnp.concatenate(both, 0)


def body(tab, object_slices, probe_wave, intensity, positions, counts):
    hbm = pl.BlockSpec(memory_space=pltpu.HBM)
    vmem = pl.BlockSpec(memory_space=pltpu.VMEM)
    dma = pltpu.SemaphoreType.DMA
    out = pl.pallas_call(
        kernel,
        out_shape=pltpu.VMEM((2, 12 * WIN), F32),
        in_specs=[hbm] * 6,
        out_specs=vmem,
        scratch_shapes=[
            pltpu.VMEM((2, 12 * WIN), BF16),
            pltpu.VMEM((24, WIN), BF16),
            pltpu.SMEM((2, 2), jnp.int32),
            pltpu.SMEM((1,), jnp.int32),
            pltpu.VMEM((2, WIN, WIN), F32),
            pltpu.VMEM((WIN, WIN), F32),
            pltpu.VMEM((5, 2, 2 * WIN, 2 * WIN), BF16),
            pltpu.VMEM((12, 24, WIN), BF16),
            pltpu.VMEM((3, 2, 3, 2, 8, WIN), F32),
            pltpu.VMEM((8, 4, WIN), jnp.int32),
            pltpu.VMEM((16, 32, WIN), BF16),
            pltpu.VMEM((8, 8, 32, WIN), BF16),
            pltpu.VMEM((8, WIN, 2 * WIN), F32),
            pltpu.VMEM((WIN, 2 * WIN), F32),
            pltpu.VMEM((64, 17, WIN), jnp.int32),
            pltpu.VMEM((2, 8, 17, WIN), jnp.int32),
            pltpu.VMEM((12, 13, WIN), jnp.int32),
            pltpu.VMEM((12, 13, WIN), jnp.int32),
            dma((6,)),
            pltpu.SemaphoreType.REGULAR((3,)),
            dma((2,)), dma((2,)),
            dma, dma((8,)),
            dma, dma,
            dma((2,)),
        ],
        compiler_params=pltpu.CompilerParams(
            collective_id=0, has_side_effects=True, vmem_limit_bytes=60 << 20
        ),
    )(object_slices, positions, counts, probe_wave, intensity, tab)
    return out.reshape(1, 2, 12 * WIN)


def solution(mesh):
    tab = tables()
    in_specs = (P("cuts", None, "scan"), P(), P("scan", None, None), P("scan", None), P("scan"))
    out_specs = P("cuts", None, "scan")
    return jax.shard_map(
        functools.partial(body, tab), mesh=mesh, in_specs=in_specs, out_specs=out_specs, check_vma=False
    )
```

```python
import functools

import jax
import jax.numpy as jnp
import ml_dtypes
import numpy as np
from jax import lax
from jax.experimental import pallas as pl
from jax.experimental.pallas import tpu as pltpu
from jax.sharding import PartitionSpec as P

WIN = 128
FRESNEL = 0.5
GRAD_SCALE = 0.25
NZ = 12
FARTHEST = (5, 7, 4, 8, 2, 10, 1, 11, 6, 3, 9)
F32 = jnp.float32
BF16 = jnp.bfloat16
MESH = pl.DeviceIdType.MESH


def row_order():
    rho = np.arange(WIN)
    q, h, k, rr = rho // 16, (rho // 8) % 2, (rho // 4) % 2, rho % 4
    return 64 * h + 32 * k + 16 * (q // 4) + 4 * (q % 4) + rr


def split_table(mat):
    hi = mat.astype(ml_dtypes.bfloat16)
    lo = (mat - hi.astype(np.float64)).astype(ml_dtypes.bfloat16)
    return np.stack([hi, lo])


def tables():
    k = np.arange(WIN)
    four = np.exp(-2j * np.pi * ((k[:, None] * k[None, :]) % WIN) / WIN) / np.sqrt(WIN)
    freq = np.where(k < WIN // 2, k, k - WIN).astype(np.float64)
    half = np.exp(-1j * np.pi * FRESNEL * freq * freq / WIN)
    kern = np.conj(four.T) @ (half[:, None] * four)
    order = row_order()

    def right(mat):
        return split_table(np.block([[mat.real, mat.imag], [-mat.imag, mat.real]]))

    def left(mat):
        return split_table(np.block([[mat.real, -mat.imag], [mat.imag, mat.real]]))

    return np.stack(
        [
            right(kern),
            left(kern[order][:, order]),
            right(four),
            left(four[:, order]),
            left(four[order]),
        ]
    )


def dot(a, b):
    return jnp.dot(a, b, preferred_element_type=F32)


def split(x):
    hi = x.astype(BF16)
    return hi, (x - hi.astype(F32)).astype(BF16)


def sandwich(x, right, left):
    hi, lo = split(x)
    both = dot(jnp.concatenate([hi, lo], 0), right[0])
    mid = both[:WIN] + both[WIN:] + dot(hi, right[1])
    mid = jnp.concatenate([mid[:, :WIN], mid[:, WIN:]], 0)
    hi, lo = split(mid)
    both = dot(left[0], jnp.concatenate([hi, lo], 1))
    out = both[:, :WIN] + both[:, WIN:] + dot(left[1], hi)
    return jnp.concatenate([out[:WIN], out[WIN:]], 1)


def complex_mul(x, w):
    x_re, x_im, w_re, w_im = x[:, :WIN], x[:, WIN:], w[:, :WIN], w[:, WIN:]
    return jnp.concatenate([x_re * w_re - x_im * w_im, x_re * w_im + x_im * w_re], 1)


def rolled_probe(probe_ref, row_at, col_at):
    shape = (WIN, WIN)
    rho = lax.broadcasted_iota(jnp.int32, shape, 0)
    lane = lax.broadcasted_iota(jnp.int32, shape, 1)
    t = (
        64 * ((rho >> 3) & 1)
        + 32 * ((rho >> 2) & 1)
        + 16 * ((rho >> 6) & 1)
        + 4 * ((rho >> 4) & 3)
        + (rho & 3)
    )
    rows = (((t - lane - row_at) & (WIN - 1)) == 0).astype(F32).astype(BF16)
    cols = (((lane - rho - col_at) & (WIN - 1)) == 0).astype(F32).astype(BF16)
    halves = []
    for plane in range(2):
        rest = probe_ref[plane]
        total = jnp.zeros(shape, F32)
        for _ in range(3):
            part = rest.astype(BF16)
            rest = rest - part.astype(F32)
            total = total + dot(dot(rows, part).astype(BF16), cols)
        halves.append(total)
    return jnp.concatenate(halves, 1)


STEPS = 256
TOP = 32760.0


def scale_of(steps):
    return jnp.exp(steps.astype(F32) * (np.log(2.0) / STEPS))


def pack(re, im, groups):
    def grouped(part):
        return part.reshape(groups, -1, 8, WIN)

    most = jnp.max(grouped(jnp.maximum(jnp.abs(re), jnp.abs(im))), axis=1)
    most = jnp.max(most, axis=1, keepdims=True)
    steps = jnp.ceil(jnp.log(jnp.maximum(most, 1e-30)) * (STEPS / np.log(2.0))).astype(jnp.int32)
    factor = (TOP * scale_of(-steps))[:, None]
    whole_re, whole_im = (jnp.floor(grouped(part) * factor + 0.5).astype(jnp.int32) for part in (re, im))
    return ((whole_re << 16) | (whole_im & 0xFFFF)).reshape(re.shape), steps


def unpack(both, steps, factor):
    scale = scale_of(steps) * (factor / TOP)
    return (both >> 16).astype(F32) * scale, ((both << 16) >> 16).astype(F32) * scale


def rem(a, b):
    return lax.rem(a, jnp.int32(b))


def div(a, b):
    return lax.div(a, jnp.int32(b))


def kernel(
    obj_ref, pos_ref, counts_ref, probe_ref, inten_ref, tab_ref,
    out_ref,
    raw, obj, pos, counts, probe, inten, tab,
    cells, strips, aux_all, pieces, win, psis, wave, esend, erecv, fsend, frecv,
    in_sems, near_sems, a_sem, p_sem, b_send, b_recv, e_send, e_recv, f_sem,
):
    cut = lax.axis_index("cuts")
    me = lax.axis_index("scan")
    x, core = div(cut, 2), rem(cut, 2)
    y, z = div(me, NZ), rem(me, NZ)
    z_block, z_in = div(z, 4), rem(z, 4)
    y_block, y_in = div(y, 2), rem(y, 2)
    bit_b = rem(y_in + z_block, 2)
    q = 4 * bit_b + z_in
    n_mine = div(me, 8)
    row_base = 16 * bit_b + 4 * z_in

    def worker(yi, zi, j):
        return rem(yi + zi + j, 2)

    working = x == worker(y_in, z_in, core)

    def far(d):
        n = rem(n_mine + d, 12)
        return n, 8 * n + 4 * bit_b + z_in

    def mate(dy, dz):
        yi, zi = rem(y_in + dy, 2), rem(z_in + dz, 4)
        return yi, zi, 4 * rem(yi + z_block, 2) + zi, (2 * y_block + yi) * NZ + 4 * z_block + zi

    def near(i):
        flag = lambda hit: jnp.asarray(hit).astype(jnp.int32)
        i = jnp.asarray(i, jnp.int32)
        other_row, same_column = flag(i < 3) + flag(i == 6), flag(i == 6)
        up = rem(i, 3)
        down = 3 - up
        upper = flag(z_in >= 2)
        column = upper * (up + flag(up >= z_in)) + (1 - upper) * (down - flag(down <= z_in))
        zi = same_column * z_in + (1 - same_column) * column
        yi = other_row * (1 - y_in) + (1 - other_row) * y_in
        return yi, zi, 4 * rem(yi + z_block, 2) + zi, (2 * y_block + yi) * NZ + 4 * z_block + zi

    def at(cut_to, scan_to):
        return dict(device_id={"cuts": cut_to, "scan": scan_to}, device_id_type=MESH)

    sibling = cut + 1 - 2 * core

    def chip_at(i):
        x_to = i + (x <= i).astype(jnp.int32)
        return 2 * x_to + core

    loads = [
        (obj_ref.at[0], raw), (pos_ref, pos), (counts_ref, counts), (probe_ref, probe), (inten_ref.at[core], inten), (tab_ref, tab),
    ]
    loads = [pltpu.make_async_copy(src, dst, in_sems.at[i]) for i, (src, dst) in enumerate(loads)]
    for load in loads:
        load.start()

    barrier = pltpu.get_barrier_semaphore()
    for d in FARTHEST:
        pl.semaphore_signal(barrier, inc=1, **at(cut, far(d)[1]))
    for d in range(1, 4):
        pl.semaphore_signal(barrier, inc=1, **at(cut, mate(0, d)[3]))
    pl.semaphore_signal(barrier, inc=1, **at(cut, mate(1, 0)[3]))
    pl.semaphore_signal(barrier, inc=1, **at(sibling, me))
    for i in range(3):
        pl.semaphore_signal(barrier, inc=1, **at(chip_at(i), me))

    loads[0].wait()
    flat_obj = raw[...].astype(F32)
    rows = []
    for c in range(3):
        for plane in range(2):
            for rr in range(4):
                first = (3 * rr + c) * WIN
                rows.append(flat_obj[plane : plane + 1, first : first + WIN])
    obj[...] = jnp.concatenate(rows, 0).astype(BF16)
    pl.semaphore_wait(barrier, 19)

    pl.semaphore_signal(near_sems.at[0], inc=1, **at(cut, mate(1, 0)[3]))

    for d in FARTHEST:
        pltpu.make_async_remote_copy(
            src_ref=obj, dst_ref=cells.at[n_mine], send_sem=a_sem.at[0], recv_sem=a_sem.at[1], **at(cut, far(d)[1])
        ).start()
    cells[n_mine] = obj[...]

    loads[1].wait()
    loads[2].wait()
    here = 4 * y_in + z_in
    sub = lax.broadcasted_iota(jnp.int32, (8, WIN), 0)
    lane = lax.broadcasted_iota(jnp.int32, (8, WIN), 1)
    mine = jnp.where(
        sub == 0, pos[0, 0], jnp.where(sub == 1, pos[0, 1], jnp.where(sub == 2, pos[1, 0], pos[1, 1]))
    )
    aux_all[here] = mine[0:4]
    pl.semaphore_wait(near_sems.at[0], 1)
    pl.semaphore_signal(near_sems.at[1], inc=1, **at(sibling, me))
    for i in range(7):
        pltpu.make_async_remote_copy(
            src_ref=aux_all.at[here], dst_ref=aux_all.at[here],
            send_sem=p_sem.at[0], recv_sem=p_sem.at[1], **at(cut, near(i)[3])
        ).start()
    pl.semaphore_wait(near_sems.at[1], 1)
    for i in range(3):
        pl.semaphore_signal(near_sems.at[2], inc=1, **at(chip_at(i), me))

    loads[3].wait()
    loads[4].wait()
    loads[5].wait()

    @pl.when(working)
    def _():
        row_at = jnp.where(core == 0, pos[0, 0], pos[1, 0])
        col_at = jnp.where(core == 0, pos[0, 1], pos[1, 1])
        wave[...] = rolled_probe(probe, row_at, col_at)

    pltpu.make_async_copy(aux_all.at[0:7], aux_all.at[0:7], p_sem.at[1]).wait()
    pl.semaphore_wait(near_sems.at[2], 3)
    pltpu.make_async_copy(cells.at[0:11], cells.at[0:11], a_sem.at[1]).wait()

    blocks = [cells[n].astype(F32) for n in range(12)]
    for third in range(3):
        for h in range(2):
            for c in range(3):
                for plane in range(2):
                    first = 8 * c + 4 * plane
                    rows = [blocks[4 * third + 2 * h + k][first : first + 4] for k in range(2)]
                    strips[third, h, c, plane] = jnp.concatenate(rows, 0)

    row_here = 32 * (sub >> 2) + (sub & 3) + row_base

    def masks(p, j):
        a = aux_all[p, 2 * j : 2 * j + 1, :]
        b = aux_all[p, 2 * j + 1 : 2 * j + 2, :]
        in_row = [[((row_here + (WIN * third + 64 * h) - a) & -WIN) == 0 for third in range(3)] for h in range(2)]
        in_col = [((lane + WIN * c - b) & -WIN) == 0 for c in range(3)]
        return in_row, in_col

    def pick(p):
        for j in range(2):
            in_row, in_col = masks(p, j)
            tiles = []
            for plane in range(2):
                for h in range(2):
                    cand = []
                    for third in range(3):
                        c0, c1, c2 = (strips[third, h, c, plane] for c in range(3))
                        cand.append(jnp.where(in_col[0], c0, jnp.where(in_col[1], c1, c2)))
                    tiles.append(jnp.where(in_row[h][0], cand[0], jnp.where(in_row[h][1], cand[1], cand[2])))
            pieces[2 * p + j] = jnp.concatenate(tiles, 0).astype(BF16)

    def piece_send(yi, zi, j, to):
        pltpu.make_async_remote_copy(
            src_ref=pieces.at[2 * (4 * yi + zi) + j], dst_ref=win.at[cut, q],
            send_sem=b_send, recv_sem=b_recv.at[cut], **at(2 * worker(yi, zi, j) + j, to)
        ).start()

    def pick_and_send(i, carry):
        yi, zi, _, to = near(i)
        pick(4 * yi + zi)
        for j in range(2):
            piece_send(yi, zi, j, to)
        return carry

    lax.fori_loop(0, 7, pick_and_send, 0)
    pick(here)
    piece_send(y_in, z_in, 1 - core, me)

    @pl.when(working)
    def _():
        pltpu.make_async_copy(pieces.at[2 * here + core], win.at[cut, q], b_recv.at[cut]).start()

    @pl.when(jnp.logical_not(working))
    def _():
        piece_send(y_in, z_in, core, me)

    def window(s):
        w = win[s].astype(F32)
        return jnp.concatenate([w[:, 0:16].reshape(WIN, WIN), w[:, 16:32].reshape(WIN, WIN)], 1)

    def pair(i):
        return (tab[i, 0], tab[i, 1])

    def arrive(s):
        pltpu.make_async_copy(win.at[s], win.at[s], b_recv.at[s]).wait()
        psi = wave[...]
        psis[s] = psi
        return complex_mul(psi, window(s))

    def forward(s, carry):
        wave[...] = sandwich(arrive(s), pair(0), pair(1))
        return carry

    def residual(last):
        far_field = sandwich(last, pair(2), pair(3))
        far_re, far_im = far_field[:, :WIN], far_field[:, WIN:]
        live = jnp.where(core < counts[0], 1.0, 0.0).astype(F32)
        excess = (far_re * far_re + far_im * far_im - inten[...]) * live
        wave[...] = sandwich(jnp.concatenate([excess * far_re, -(excess * far_im)], 1), pair(2), pair(4))

    def send_gradient(s, u):
        g = complex_mul(psis[s], u)
        both, steps = pack(g[:, :WIN].reshape(8, 16, WIN), -g[:, WIN:].reshape(8, 16, WIN), 4)
        steps = jnp.broadcast_to(steps[:, None], (4, 2, 1, WIN)).reshape(8, 1, WIN)
        esend[pl.ds(8 * s, 8)] = jnp.concatenate([both, steps], 1)
        for i in range(7):
            send_one(s, *near(i)[2:])

    def send_one(s, q_to, to):
        pltpu.make_async_remote_copy(
            src_ref=esend.at[8 * s + q_to], dst_ref=erecv.at[core, here],
            send_sem=e_send, recv_sem=e_recv, **at(s, to)
        ).start()

    def send_own(s):
        @pl.when(s != cut)
        def _():
            send_one(s, q, me)

        @pl.when(s == cut)
        def _():
            pltpu.make_async_copy(esend.at[8 * s + q], erecv.at[core, here], e_recv).start()

    def backward(n, carry):
        s = 7 - n
        u = wave[...]
        send_gradient(s, u)
        wave[...] = sandwich(complex_mul(u, window(s)), pair(0), pair(1))
        send_own(s)
        return carry

    @pl.when(working)
    def _():
        lax.fori_loop(0, 7, forward, 0)
        residual(arrive(7))
        lax.fori_loop(0, 7, backward, 0)
        send_gradient(0, wave[...])
        send_own(0)

    pltpu.make_async_copy(erecv, erecv, e_recv).wait()

    def place(p, sums):
        sums = list(sums)
        for j in range(2):
            in_row, in_col = masks(p, j)
            vals = unpack(erecv[j, p, 0:16, :], erecv[j, p, 16:17, :], 1.0)
            for plane in range(2):
                for h in range(2):
                    val = vals[plane][8 * h : 8 * h + 8]
                    for third in range(3):
                        kept = jnp.where(in_row[h][third], val, 0.0)
                        for c in range(3):
                            i = ((third * 2 + h) * 3 + c) * 2 + plane
                            sums[i] = sums[i] + jnp.where(in_col[c], kept, 0.0)
        return tuple(sums)

    sums = lax.fori_loop(0, 8, place, tuple(jnp.zeros((8, WIN), F32) for _ in range(36)))
    for half in range(6):
        re, im = (jnp.stack([sums[(half * 3 + c) * 2 + plane] for c in range(3)]) for plane in range(2))
        both, steps = pack(re, im, 1)
        for k in range(2):
            rows = [both[c, 4 * k : 4 * k + 4] for c in range(3)] + [steps[0]]
            fsend[2 * half + k] = jnp.concatenate(rows, 0)

    for d in FARTHEST:
        n_to, to = far(d)
        pltpu.make_async_remote_copy(
            src_ref=fsend.at[n_to], dst_ref=frecv.at[n_mine], send_sem=f_sem.at[0], recv_sem=f_sem.at[1], **at(cut, to)
        ).start()
    frecv[n_mine] = fsend[n_mine]

    @pl.when(working)
    def _():
        pltpu.make_async_copy(pieces.at[0:15], pieces.at[0:15], b_send).wait()
        pltpu.make_async_copy(esend.at[0:63], esend.at[0:63], e_send).wait()

    @pl.when(jnp.logical_not(working))
    def _():
        pltpu.make_async_copy(pieces, pieces, b_send).wait()

    for ref, sem in (
        (cells.at[0:11], a_sem.at[0]),
        (aux_all.at[0:7], p_sem.at[0]),
        (fsend.at[0:11], f_sem.at[0]),
        (frecv.at[0:11], f_sem.at[1]),
    ):
        pltpu.make_async_copy(ref, ref, sem).wait()
    total = [jnp.zeros((12, WIN), F32)] * 2
    for n in range(12):
        part = unpack(frecv[n, 0:12, :], frecv[n, 12:13, :], GRAD_SCALE)
        total = [total[plane] + part[plane] for plane in range(2)]
    for rr in range(4):
        for c in range(3):
            first = (3 * rr + c) * WIN
            both = [total[plane][4 * c + rr : 4 * c + rr + 1] for plane in range(2)]
            out_ref[:, first : first + WIN] = jnp.concatenate(both, 0)


def body(tab, object_slices, probe_wave, intensity, positions, counts):
    hbm = pl.BlockSpec(memory_space=pltpu.HBM)
    vmem = pl.BlockSpec(memory_space=pltpu.VMEM)
    dma = pltpu.SemaphoreType.DMA
    out = pl.pallas_call(
        kernel,
        out_shape=pltpu.VMEM((2, 12 * WIN), F32),
        in_specs=[hbm] * 6,
        out_specs=vmem,
        scratch_shapes=[
            pltpu.VMEM((2, 12 * WIN), BF16),
            pltpu.VMEM((24, WIN), BF16),
            pltpu.SMEM((2, 2), jnp.int32),
            pltpu.SMEM((1,), jnp.int32),
            pltpu.VMEM((2, WIN, WIN), F32),
            pltpu.VMEM((WIN, WIN), F32),
            pltpu.VMEM((5, 2, 2 * WIN, 2 * WIN), BF16),
            pltpu.VMEM((12, 24, WIN), BF16),
            pltpu.VMEM((3, 2, 3, 2, 8, WIN), F32),
            pltpu.VMEM((8, 4, WIN), jnp.int32),
            pltpu.VMEM((16, 32, WIN), BF16),
            pltpu.VMEM((8, 8, 32, WIN), BF16),
            pltpu.VMEM((8, WIN, 2 * WIN), F32),
            pltpu.VMEM((WIN, 2 * WIN), F32),
            pltpu.VMEM((64, 17, WIN), jnp.int32),
            pltpu.VMEM((2, 8, 17, WIN), jnp.int32),
            pltpu.VMEM((12, 13, WIN), jnp.int32),
            pltpu.VMEM((12, 13, WIN), jnp.int32),
            dma((6,)),
            pltpu.SemaphoreType.REGULAR((3,)),
            dma((2,)), dma((2,)),
            dma, dma((8,)),
            dma, dma,
            dma((2,)),
        ],
        compiler_params=pltpu.CompilerParams(
            collective_id=0, has_side_effects=True, vmem_limit_bytes=60 << 20
        ),
    )(object_slices, positions, counts, probe_wave, intensity, tab)
    return out.reshape(1, 2, 12 * WIN)


def solution(mesh):
    tab = tables()
    in_specs = (P("cuts", None, "scan"), P(), P("scan", None, None), P("scan", None), P("scan"))
    out_specs = P("cuts", None, "scan")
    return jax.shard_map(
        functools.partial(body, tab), mesh=mesh, in_specs=in_specs, out_specs=out_specs, check_vma=False
    )
```

```python
import functools

import jax
import jax.numpy as jnp
import ml_dtypes
import numpy as np
from jax import lax
from jax.experimental import pallas as pl
from jax.experimental.pallas import tpu as pltpu
from jax.sharding import PartitionSpec as P

WIN = 128
FRESNEL = 0.5
GRAD_SCALE = 0.25
NZ = 12
FARTHEST = (5, 7, 4, 8, 2, 10, 1, 11, 6, 3, 9)
F32 = jnp.float32
BF16 = jnp.bfloat16
MESH = pl.DeviceIdType.MESH


def row_order():
    rho = np.arange(WIN)
    q, h, k, rr = rho // 16, (rho // 8) % 2, (rho // 4) % 2, rho % 4
    return 64 * h + 32 * k + 16 * (q // 4) + 4 * (q % 4) + rr


def split_table(mat):
    hi = mat.astype(ml_dtypes.bfloat16)
    lo = (mat - hi.astype(np.float64)).astype(ml_dtypes.bfloat16)
    return np.stack([hi, lo])


def tables():
    k = np.arange(WIN)
    four = np.exp(-2j * np.pi * ((k[:, None] * k[None, :]) % WIN) / WIN) / np.sqrt(WIN)
    freq = np.where(k < WIN // 2, k, k - WIN).astype(np.float64)
    half = np.exp(-1j * np.pi * FRESNEL * freq * freq / WIN)
    kern = np.conj(four.T) @ (half[:, None] * four)
    order = row_order()

    def right(mat):
        return split_table(np.block([[mat.real, mat.imag], [-mat.imag, mat.real]]))

    def left(mat):
        return split_table(np.block([[mat.real, -mat.imag], [mat.imag, mat.real]]))

    return np.stack(
        [
            right(kern),
            left(kern[order][:, order]),
            right(four),
            left(four[:, order]),
            left(four[order]),
        ]
    )


def dot(a, b):
    return jnp.dot(a, b, preferred_element_type=F32)


def split(x):
    hi = x.astype(BF16)
    return hi, (x - hi.astype(F32)).astype(BF16)


def sandwich(x, right, left):
    hi, lo = split(x)
    both = dot(jnp.concatenate([hi, lo], 0), right[0])
    mid = both[:WIN] + both[WIN:] + dot(hi, right[1])
    mid = jnp.concatenate([mid[:, :WIN], mid[:, WIN:]], 0)
    hi, lo = split(mid)
    both = dot(left[0], jnp.concatenate([hi, lo], 1))
    out = both[:, :WIN] + both[:, WIN:] + dot(left[1], hi)
    return jnp.concatenate([out[:WIN], out[WIN:]], 1)


def complex_mul(x, w):
    x_re, x_im, w_re, w_im = x[:, :WIN], x[:, WIN:], w[:, :WIN], w[:, WIN:]
    return jnp.concatenate([x_re * w_re - x_im * w_im, x_re * w_im + x_im * w_re], 1)


def rolled_probe(probe_ref, row_at, col_at):
    shape = (WIN, WIN)
    rho = lax.broadcasted_iota(jnp.int32, shape, 0)
    lane = lax.broadcasted_iota(jnp.int32, shape, 1)
    t = (
        64 * ((rho >> 3) & 1)
        + 32 * ((rho >> 2) & 1)
        + 16 * ((rho >> 6) & 1)
        + 4 * ((rho >> 4) & 3)
        + (rho & 3)
    )
    rows = (((t - lane - row_at) & (WIN - 1)) == 0).astype(F32).astype(BF16)
    cols = (((lane - rho - col_at) & (WIN - 1)) == 0).astype(F32).astype(BF16)
    halves = []
    for plane in range(2):
        rest = probe_ref[plane]
        total = jnp.zeros(shape, F32)
        for _ in range(3):
            part = rest.astype(BF16)
            rest = rest - part.astype(F32)
            total = total + dot(dot(rows, part).astype(BF16), cols)
        halves.append(total)
    return jnp.concatenate(halves, 1)


STEPS = 256
TOP = 32760.0


def scale_of(steps):
    return jnp.exp(steps.astype(F32) * (np.log(2.0) / STEPS))


def pack(re, im, groups):
    def grouped(part):
        return part.reshape(groups, -1, 8, WIN)

    most = jnp.max(grouped(jnp.maximum(jnp.abs(re), jnp.abs(im))), axis=1)
    most = jnp.max(most, axis=1, keepdims=True)
    steps = jnp.ceil(jnp.log(jnp.maximum(most, 1e-30)) * (STEPS / np.log(2.0))).astype(jnp.int32)
    factor = (TOP * scale_of(-steps))[:, None]
    whole_re, whole_im = (jnp.floor(grouped(part) * factor + 0.5).astype(jnp.int32) for part in (re, im))
    return ((whole_re << 16) | (whole_im & 0xFFFF)).reshape(re.shape), steps


def unpack(both, steps, factor):
    scale = scale_of(steps) * (factor / TOP)
    return (both >> 16).astype(F32) * scale, ((both << 16) >> 16).astype(F32) * scale


def rem(a, b):
    return lax.rem(a, jnp.int32(b))


def div(a, b):
    return lax.div(a, jnp.int32(b))


def kernel(
    obj_ref, pos_ref, counts_ref, probe_ref, inten_ref, tab_ref,
    out_ref,
    raw, obj, pos, counts, probe, inten, tab,
    cells, strips, aux_all, pieces, win, psis, wave, esend, erecv, fsend, frecv,
    in_sems, near_sems, a_sem, p_sem, b_send, b_recv, e_send, e_recv, f_sem,
):
    cut = lax.axis_index("cuts")
    me = lax.axis_index("scan")
    x, core = div(cut, 2), rem(cut, 2)
    y, z = div(me, NZ), rem(me, NZ)
    z_block, z_in = div(z, 4), rem(z, 4)
    y_block, y_in = div(y, 2), rem(y, 2)
    bit_b = rem(y_in + z_block, 2)
    q = 4 * bit_b + z_in
    n_mine = div(me, 8)
    row_base = 16 * bit_b + 4 * z_in

    def worker(yi, zi, j):
        return rem(yi + zi + j, 2)

    working = x == worker(y_in, z_in, core)

    def far(d):
        n = rem(n_mine + d, 12)
        return n, 8 * n + 4 * bit_b + z_in

    def mate(dy, dz):
        yi, zi = rem(y_in + dy, 2), rem(z_in + dz, 4)
        return yi, zi, 4 * rem(yi + z_block, 2) + zi, (2 * y_block + yi) * NZ + 4 * z_block + zi

    def near(i):
        flag = lambda hit: jnp.asarray(hit).astype(jnp.int32)
        i = jnp.asarray(i, jnp.int32)
        other_row, same_column = flag(i < 3) + flag(i == 6), flag(i == 6)
        up = rem(i, 3)
        down = 3 - up
        upper = flag(z_in >= 2)
        column = upper * (up + flag(up >= z_in)) + (1 - upper) * (down - flag(down <= z_in))
        zi = same_column * z_in + (1 - same_column) * column
        yi = other_row * (1 - y_in) + (1 - other_row) * y_in
        return yi, zi, 4 * rem(yi + z_block, 2) + zi, (2 * y_block + yi) * NZ + 4 * z_block + zi

    def at(cut_to, scan_to):
        return dict(device_id={"cuts": cut_to, "scan": scan_to}, device_id_type=MESH)

    sibling = cut + 1 - 2 * core

    def chip_at(i):
        x_to = i + (x <= i).astype(jnp.int32)
        return 2 * x_to + core

    loads = [
        (obj_ref.at[0], raw), (pos_ref, pos), (counts_ref, counts), (probe_ref, probe), (inten_ref.at[core], inten), (tab_ref, tab),
    ]
    loads = [pltpu.make_async_copy(src, dst, in_sems.at[i]) for i, (src, dst) in enumerate(loads)]
    for load in loads:
        load.start()

    barrier = pltpu.get_barrier_semaphore()
    for d in FARTHEST:
        pl.semaphore_signal(barrier, inc=1, **at(cut, far(d)[1]))
    for d in range(1, 4):
        pl.semaphore_signal(barrier, inc=1, **at(cut, mate(0, d)[3]))
    pl.semaphore_signal(barrier, inc=1, **at(cut, mate(1, 0)[3]))
    pl.semaphore_signal(barrier, inc=1, **at(sibling, me))
    for i in range(3):
        pl.semaphore_signal(barrier, inc=1, **at(chip_at(i), me))

    loads[0].wait()
    flat_obj = raw[...].astype(F32)
    rows = []
    for c in range(3):
        for plane in range(2):
            for rr in range(4):
                first = (3 * rr + c) * WIN
                rows.append(flat_obj[plane : plane + 1, first : first + WIN])
    obj[...] = jnp.concatenate(rows, 0).astype(BF16)
    pl.semaphore_wait(barrier, 19)

    pl.semaphore_signal(near_sems.at[0], inc=1, **at(cut, mate(1, 0)[3]))

    for d in FARTHEST:
        pltpu.make_async_remote_copy(
            src_ref=obj, dst_ref=cells.at[n_mine], send_sem=a_sem.at[0], recv_sem=a_sem.at[1], **at(cut, far(d)[1])
        ).start()
    cells[n_mine] = obj[...]

    loads[1].wait()
    loads[2].wait()
    here = 4 * y_in + z_in
    sub = lax.broadcasted_iota(jnp.int32, (8, WIN), 0)
    lane = lax.broadcasted_iota(jnp.int32, (8, WIN), 1)
    mine = jnp.where(
        sub == 0, pos[0, 0], jnp.where(sub == 1, pos[0, 1], jnp.where(sub == 2, pos[1, 0], pos[1, 1]))
    )
    aux_all[here] = mine[0:4]
    pl.semaphore_wait(near_sems.at[0], 1)
    pl.semaphore_signal(near_sems.at[1], inc=1, **at(sibling, me))
    for i in range(7):
        pltpu.make_async_remote_copy(
            src_ref=aux_all.at[here], dst_ref=aux_all.at[here],
            send_sem=p_sem.at[0], recv_sem=p_sem.at[1], **at(cut, near(i)[3])
        ).start()
    pl.semaphore_wait(near_sems.at[1], 1)
    for i in range(3):
        pl.semaphore_signal(near_sems.at[2], inc=1, **at(chip_at(i), me))

    loads[3].wait()
    loads[4].wait()
    loads[5].wait()

    @pl.when(working)
    def _():
        row_at = jnp.where(core == 0, pos[0, 0], pos[1, 0])
        col_at = jnp.where(core == 0, pos[0, 1], pos[1, 1])
        wave[...] = rolled_probe(probe, row_at, col_at)

    pltpu.make_async_copy(aux_all.at[0:7], aux_all.at[0:7], p_sem.at[1]).wait()
    pl.semaphore_wait(near_sems.at[2], 3)
    pltpu.make_async_copy(cells.at[0:11], cells.at[0:11], a_sem.at[1]).wait()

    blocks = [cells[n].astype(F32) for n in range(12)]
    for third in range(3):
        for h in range(2):
            for c in range(3):
                for plane in range(2):
                    first = 8 * c + 4 * plane
                    rows = [blocks[4 * third + 2 * h + k][first : first + 4] for k in range(2)]
                    strips[third, h, c, plane] = jnp.concatenate(rows, 0)

    row_here = 32 * (sub >> 2) + (sub & 3) + row_base

    def masks(p, j):
        a = aux_all[p, 2 * j : 2 * j + 1, :]
        b = aux_all[p, 2 * j + 1 : 2 * j + 2, :]
        in_row = [[((row_here + (WIN * third + 64 * h) - a) & -WIN) == 0 for third in range(3)] for h in range(2)]
        in_col = [((lane + WIN * c - b) & -WIN) == 0 for c in range(3)]
        return in_row, in_col

    def pick(p):
        for j in range(2):
            in_row, in_col = masks(p, j)
            tiles = []
            for plane in range(2):
                for h in range(2):
                    cand = []
                    for third in range(3):
                        c0, c1, c2 = (strips[third, h, c, plane] for c in range(3))
                        cand.append(jnp.where(in_col[0], c0, jnp.where(in_col[1], c1, c2)))
                    tiles.append(jnp.where(in_row[h][0], cand[0], jnp.where(in_row[h][1], cand[1], cand[2])))
            pieces[2 * p + j] = jnp.concatenate(tiles, 0).astype(BF16)

    def piece_send(yi, zi, j, to):
        pltpu.make_async_remote_copy(
            src_ref=pieces.at[2 * (4 * yi + zi) + j], dst_ref=win.at[cut, q],
            send_sem=b_send, recv_sem=b_recv.at[cut], **at(2 * worker(yi, zi, j) + j, to)
        ).start()

    def pick_and_send(i, carry):
        yi, zi, _, to = near(i)
        pick(4 * yi + zi)
        for j in range(2):
            pl.when(worker(yi, zi, j) != x)(functools.partial(piece_send, yi, zi, j, to))
        return carry

    def send_here(i, carry):
        yi, zi, _, to = near(i)
        for j in range(2):
            pl.when(worker(yi, zi, j) == x)(functools.partial(piece_send, yi, zi, j, to))
        return carry

    lax.fori_loop(0, 7, pick_and_send, 0)
    lax.fori_loop(0, 7, send_here, 0)
    pick(here)
    piece_send(y_in, z_in, 1 - core, me)

    @pl.when(working)
    def _():
        pltpu.make_async_copy(pieces.at[2 * here + core], win.at[cut, q], b_recv.at[cut]).start()

    @pl.when(jnp.logical_not(working))
    def _():
        piece_send(y_in, z_in, core, me)

    def window(s):
        w = win[s].astype(F32)
        return jnp.concatenate([w[:, 0:16].reshape(WIN, WIN), w[:, 16:32].reshape(WIN, WIN)], 1)

    def pair(i):
        return (tab[i, 0], tab[i, 1])

    def arrive(s):
        pltpu.make_async_copy(win.at[s], win.at[s], b_recv.at[s]).wait()
        psi = wave[...]
        psis[s] = psi
        return complex_mul(psi, window(s))

    def forward(s, carry):
        wave[...] = sandwich(arrive(s), pair(0), pair(1))
        return carry

    def residual(last):
        far_field = sandwich(last, pair(2), pair(3))
        far_re, far_im = far_field[:, :WIN], far_field[:, WIN:]
        live = jnp.where(core < counts[0], 1.0, 0.0).astype(F32)
        excess = (far_re * far_re + far_im * far_im - inten[...]) * live
        wave[...] = sandwich(jnp.concatenate([excess * far_re, -(excess * far_im)], 1), pair(2), pair(4))

    def send_gradient(s, u):
        g = complex_mul(psis[s], u)
        both, steps = pack(g[:, :WIN].reshape(8, 16, WIN), -g[:, WIN:].reshape(8, 16, WIN), 4)
        steps = jnp.broadcast_to(steps[:, None], (4, 2, 1, WIN)).reshape(8, 1, WIN)
        esend[pl.ds(8 * s, 8)] = jnp.concatenate([both, steps], 1)
        for i in range(7):
            send_one(s, *near(i)[2:])

    def send_one(s, q_to, to):
        pltpu.make_async_remote_copy(
            src_ref=esend.at[8 * s + q_to], dst_ref=erecv.at[core, here],
            send_sem=e_send, recv_sem=e_recv, **at(s, to)
        ).start()

    def send_own(s):
        @pl.when(s != cut)
        def _():
            send_one(s, q, me)

        @pl.when(s == cut)
        def _():
            pltpu.make_async_copy(esend.at[8 * s + q], erecv.at[core, here], e_recv).start()

    def backward(n, carry):
        s = 7 - n
        u = wave[...]
        send_gradient(s, u)
        wave[...] = sandwich(complex_mul(u, window(s)), pair(0), pair(1))
        send_own(s)
        return carry

    @pl.when(working)
    def _():
        lax.fori_loop(0, 7, forward, 0)
        residual(arrive(7))
        lax.fori_loop(0, 7, backward, 0)
        send_gradient(0, wave[...])
        send_own(0)

    pltpu.make_async_copy(erecv, erecv, e_recv).wait()

    def place(h, p, sums):
        sums = list(sums)
        for j in range(2):
            in_row, in_col = masks(p, j)
            vals = unpack(erecv[j, p, 8 * h : 8 * h + 8, :], erecv[j, p, 16:17, :], 1.0)
            for plane in range(2):
                for third in range(3):
                    kept = jnp.where(in_row[h][third], vals[plane], 0.0)
                    for c in range(3):
                        i = (third * 3 + c) * 2 + plane
                        sums[i] = sums[i] + jnp.where(in_col[c], kept, 0.0)
        return tuple(sums)

    def send_sum(n_to):
        pltpu.make_async_remote_copy(
            src_ref=fsend.at[n_to], dst_ref=frecv.at[n_mine], send_sem=f_sem.at[0], recv_sem=f_sem.at[1],
            **at(cut, 8 * n_to + 4 * bit_b + z_in)
        ).start()

    for h in range(2):
        sums = tuple(jnp.zeros((8, WIN), F32) for _ in range(18))
        sums = lax.fori_loop(0, 8, functools.partial(place, h), sums)
        for third in range(3):
            re, im = (jnp.stack([sums[(third * 3 + c) * 2 + plane] for c in range(3)]) for plane in range(2))
            both, steps = pack(re, im, 1)
            for k in range(2):
                rows = [both[c, 4 * k : 4 * k + 4] for c in range(3)] + [steps[0]]
                fsend[4 * third + 2 * h + k] = jnp.concatenate(rows, 0)
        for third in range(3):
            for k in range(2):
                n_to = 4 * third + 2 * h + k
                pl.when(n_to != n_mine)(functools.partial(send_sum, n_to))
    frecv[n_mine] = fsend[n_mine]

    @pl.when(working)
    def _():
        pltpu.make_async_copy(pieces.at[0:15], pieces.at[0:15], b_send).wait()
        pltpu.make_async_copy(esend.at[0:63], esend.at[0:63], e_send).wait()

    @pl.when(jnp.logical_not(working))
    def _():
        pltpu.make_async_copy(pieces, pieces, b_send).wait()

    for ref, sem in (
        (cells.at[0:11], a_sem.at[0]),
        (aux_all.at[0:7], p_sem.at[0]),
        (fsend.at[0:11], f_sem.at[0]),
        (frecv.at[0:11], f_sem.at[1]),
    ):
        pltpu.make_async_copy(ref, ref, sem).wait()
    total = [jnp.zeros((12, WIN), F32)] * 2
    for n in range(12):
        part = unpack(frecv[n, 0:12, :], frecv[n, 12:13, :], GRAD_SCALE)
        total = [total[plane] + part[plane] for plane in range(2)]
    for rr in range(4):
        for c in range(3):
            first = (3 * rr + c) * WIN
            both = [total[plane][4 * c + rr : 4 * c + rr + 1] for plane in range(2)]
            out_ref[:, first : first + WIN] = jnp.concatenate(both, 0)


def body(tab, object_slices, probe_wave, intensity, positions, counts):
    hbm = pl.BlockSpec(memory_space=pltpu.HBM)
    vmem = pl.BlockSpec(memory_space=pltpu.VMEM)
    dma = pltpu.SemaphoreType.DMA
    out = pl.pallas_call(
        kernel,
        out_shape=pltpu.VMEM((2, 12 * WIN), F32),
        in_specs=[hbm] * 6,
        out_specs=vmem,
        scratch_shapes=[
            pltpu.VMEM((2, 12 * WIN), BF16),
            pltpu.VMEM((24, WIN), BF16),
            pltpu.SMEM((2, 2), jnp.int32),
            pltpu.SMEM((1,), jnp.int32),
            pltpu.VMEM((2, WIN, WIN), F32),
            pltpu.VMEM((WIN, WIN), F32),
            pltpu.VMEM((5, 2, 2 * WIN, 2 * WIN), BF16),
            pltpu.VMEM((12, 24, WIN), BF16),
            pltpu.VMEM((3, 2, 3, 2, 8, WIN), F32),
            pltpu.VMEM((8, 4, WIN), jnp.int32),
            pltpu.VMEM((16, 32, WIN), BF16),
            pltpu.VMEM((8, 8, 32, WIN), BF16),
            pltpu.VMEM((8, WIN, 2 * WIN), F32),
            pltpu.VMEM((WIN, 2 * WIN), F32),
            pltpu.VMEM((64, 17, WIN), jnp.int32),
            pltpu.VMEM((2, 8, 17, WIN), jnp.int32),
            pltpu.VMEM((12, 13, WIN), jnp.int32),
            pltpu.VMEM((12, 13, WIN), jnp.int32),
            dma((6,)),
            pltpu.SemaphoreType.REGULAR((3,)),
            dma((2,)), dma((2,)),
            dma, dma((8,)),
            dma, dma,
            dma((2,)),
        ],
        compiler_params=pltpu.CompilerParams(
            collective_id=0, has_side_effects=True, vmem_limit_bytes=60 << 20
        ),
    )(object_slices, positions, counts, probe_wave, intensity, tab)
    return out.reshape(1, 2, 12 * WIN)


def solution(mesh):
    tab = tables()
    in_specs = (P("cuts", None, "scan"), P(), P("scan", None, None), P("scan", None), P("scan"))
    out_specs = P("cuts", None, "scan")
    return jax.shard_map(
        functools.partial(body, tab), mesh=mesh, in_specs=in_specs, out_specs=out_specs, check_vma=False
    )
```

```python
import functools

import jax
import jax.numpy as jnp
import ml_dtypes
import numpy as np
from jax import lax
from jax.experimental import pallas as pl
from jax.experimental.pallas import tpu as pltpu
from jax.sharding import PartitionSpec as P

WIN = 128
FRESNEL = 0.5
GRAD_SCALE = 0.25
NZ = 12
FARTHEST = (5, 7, 4, 8, 2, 10, 1, 11, 6, 3, 9)
F32 = jnp.float32
BF16 = jnp.bfloat16
MESH = pl.DeviceIdType.MESH


def row_order():
    rho = np.arange(WIN)
    q, h, k, rr = rho // 16, (rho // 8) % 2, (rho // 4) % 2, rho % 4
    return 64 * h + 32 * k + 16 * (q // 4) + 4 * (q % 4) + rr


def split_table(mat):
    hi = mat.astype(ml_dtypes.bfloat16)
    lo = (mat - hi.astype(np.float64)).astype(ml_dtypes.bfloat16)
    return np.stack([hi, lo])


def tables():
    k = np.arange(WIN)
    four = np.exp(-2j * np.pi * ((k[:, None] * k[None, :]) % WIN) / WIN) / np.sqrt(WIN)
    freq = np.where(k < WIN // 2, k, k - WIN).astype(np.float64)
    half = np.exp(-1j * np.pi * FRESNEL * freq * freq / WIN)
    kern = np.conj(four.T) @ (half[:, None] * four)
    order = row_order()

    def right(mat):
        return split_table(np.block([[mat.real, mat.imag], [-mat.imag, mat.real]]))

    def left(mat):
        return split_table(np.block([[mat.real, -mat.imag], [mat.imag, mat.real]]))

    return np.stack(
        [
            right(kern),
            left(kern[order][:, order]),
            right(four),
            left(four[:, order]),
            left(four[order]),
        ]
    )


def dot(a, b):
    return jnp.dot(a, b, preferred_element_type=F32)


def split(x):
    hi = x.astype(BF16)
    return hi, (x - hi.astype(F32)).astype(BF16)


def sandwich(x, right, left):
    hi, lo = split(x)
    both = dot(jnp.concatenate([hi, lo], 0), right[0])
    mid = both[:WIN] + both[WIN:] + dot(hi, right[1])
    mid = jnp.concatenate([mid[:, :WIN], mid[:, WIN:]], 0)
    hi, lo = split(mid)
    both = dot(left[0], jnp.concatenate([hi, lo], 1))
    out = both[:, :WIN] + both[:, WIN:] + dot(left[1], hi)
    return jnp.concatenate([out[:WIN], out[WIN:]], 1)


def complex_mul(x, w):
    x_re, x_im, w_re, w_im = x[:, :WIN], x[:, WIN:], w[:, :WIN], w[:, WIN:]
    return jnp.concatenate([x_re * w_re - x_im * w_im, x_re * w_im + x_im * w_re], 1)


def rolled_probe(probe_ref, row_at, col_at):
    shape = (WIN, WIN)
    rho = lax.broadcasted_iota(jnp.int32, shape, 0)
    lane = lax.broadcasted_iota(jnp.int32, shape, 1)
    t = (
        64 * ((rho >> 3) & 1)
        + 32 * ((rho >> 2) & 1)
        + 16 * ((rho >> 6) & 1)
        + 4 * ((rho >> 4) & 3)
        + (rho & 3)
    )
    rows = (((t - lane - row_at) & (WIN - 1)) == 0).astype(F32).astype(BF16)
    cols = (((lane - rho - col_at) & (WIN - 1)) == 0).astype(F32).astype(BF16)
    halves = []
    for plane in range(2):
        rest = probe_ref[plane]
        total = jnp.zeros(shape, F32)
        for _ in range(3):
            part = rest.astype(BF16)
            rest = rest - part.astype(F32)
            total = total + dot(dot(rows, part).astype(BF16), cols)
        halves.append(total)
    return jnp.concatenate(halves, 1)


STEPS = 256
TOP = 32760.0


def scale_of(steps):
    return jnp.exp(steps.astype(F32) * (np.log(2.0) / STEPS))


def pack(re, im, groups):
    def grouped(part):
        return part.reshape(groups, -1, 8, WIN)

    most = jnp.max(grouped(jnp.maximum(jnp.abs(re), jnp.abs(im))), axis=1)
    most = jnp.max(most, axis=1, keepdims=True)
    steps = jnp.ceil(jnp.log(jnp.maximum(most, 1e-30)) * (STEPS / np.log(2.0))).astype(jnp.int32)
    factor = (TOP * scale_of(-steps))[:, None]
    whole_re, whole_im = (jnp.floor(grouped(part) * factor + 0.5).astype(jnp.int32) for part in (re, im))
    return ((whole_re << 16) | (whole_im & 0xFFFF)).reshape(re.shape), steps


def unpack(both, steps, factor):
    scale = scale_of(steps) * (factor / TOP)
    return (both >> 16).astype(F32) * scale, ((both << 16) >> 16).astype(F32) * scale


def rem(a, b):
    return lax.rem(a, jnp.int32(b))


def div(a, b):
    return lax.div(a, jnp.int32(b))


def kernel(
    obj_ref, pos_ref, counts_ref, probe_ref, inten_ref, tab_ref,
    out_ref,
    raw, obj, pos, counts, probe, inten, tab,
    cells, strips, aux_all, pieces, win, psis, wave, esend, erecv, fsend, frecv,
    in_sems, near_sems, a_sem, p_sem, b_send, b_recv, e_send, e_recv, f_sem,
):
    cut = lax.axis_index("cuts")
    me = lax.axis_index("scan")
    x, core = div(cut, 2), rem(cut, 2)
    y, z = div(me, NZ), rem(me, NZ)
    z_block, z_in = div(z, 4), rem(z, 4)
    y_block, y_in = div(y, 2), rem(y, 2)
    bit_b = rem(y_in + z_block, 2)
    q = 4 * bit_b + z_in
    n_mine = div(me, 8)
    row_base = 16 * bit_b + 4 * z_in

    def worker(yi, zi, j):
        return rem(yi + zi + j, 2)

    working = x == worker(y_in, z_in, core)

    def far(d):
        n = rem(n_mine + d, 12)
        return n, 8 * n + 4 * bit_b + z_in

    def mate(dy, dz):
        yi, zi = rem(y_in + dy, 2), rem(z_in + dz, 4)
        return yi, zi, 4 * rem(yi + z_block, 2) + zi, (2 * y_block + yi) * NZ + 4 * z_block + zi

    def near(i):
        flag = lambda hit: jnp.asarray(hit).astype(jnp.int32)
        i = jnp.asarray(i, jnp.int32)
        other_row, same_column = flag(i < 3) + flag(i == 6), flag(i == 6)
        up = rem(i, 3)
        down = 3 - up
        upper = flag(z_in >= 2)
        column = upper * (up + flag(up >= z_in)) + (1 - upper) * (down - flag(down <= z_in))
        zi = same_column * z_in + (1 - same_column) * column
        yi = other_row * (1 - y_in) + (1 - other_row) * y_in
        return yi, zi, 4 * rem(yi + z_block, 2) + zi, (2 * y_block + yi) * NZ + 4 * z_block + zi

    def at(cut_to, scan_to):
        return dict(device_id={"cuts": cut_to, "scan": scan_to}, device_id_type=MESH)

    sibling = cut + 1 - 2 * core

    def chip_at(i):
        x_to = i + (x <= i).astype(jnp.int32)
        return 2 * x_to + core

    loads = [
        (obj_ref.at[0], raw), (pos_ref, pos), (counts_ref, counts), (probe_ref, probe), (inten_ref.at[core], inten), (tab_ref, tab),
    ]
    loads = [pltpu.make_async_copy(src, dst, in_sems.at[i]) for i, (src, dst) in enumerate(loads)]
    for load in loads:
        load.start()

    barrier = pltpu.get_barrier_semaphore()
    for d in FARTHEST:
        pl.semaphore_signal(barrier, inc=1, **at(cut, far(d)[1]))
    for d in range(1, 4):
        pl.semaphore_signal(barrier, inc=1, **at(cut, mate(0, d)[3]))
    pl.semaphore_signal(barrier, inc=1, **at(cut, mate(1, 0)[3]))
    pl.semaphore_signal(barrier, inc=1, **at(sibling, me))
    for i in range(3):
        pl.semaphore_signal(barrier, inc=1, **at(chip_at(i), me))

    loads[0].wait()
    flat_obj = raw[...].astype(F32)
    rows = []
    for c in range(3):
        for plane in range(2):
            for rr in range(4):
                first = (3 * rr + c) * WIN
                rows.append(flat_obj[plane : plane + 1, first : first + WIN])
    obj[...] = jnp.concatenate(rows + [jnp.zeros((8, WIN), F32)], 0).astype(BF16)
    pl.semaphore_wait(barrier, 19)

    pl.semaphore_signal(near_sems.at[0], inc=1, **at(cut, mate(1, 0)[3]))

    for d in FARTHEST:
        pltpu.make_async_remote_copy(
            src_ref=obj, dst_ref=cells.at[n_mine], send_sem=a_sem.at[0], recv_sem=a_sem.at[1], **at(cut, far(d)[1])
        ).start()
    cells[n_mine] = obj[...]

    loads[1].wait()
    loads[2].wait()
    here = 4 * y_in + z_in
    sub = lax.broadcasted_iota(jnp.int32, (8, WIN), 0)
    lane = lax.broadcasted_iota(jnp.int32, (8, WIN), 1)
    mine = jnp.where(
        sub == 0, pos[0, 0], jnp.where(sub == 1, pos[0, 1], jnp.where(sub == 2, pos[1, 0], pos[1, 1]))
    )
    aux_all[here] = mine[0:4]
    pl.semaphore_wait(near_sems.at[0], 1)
    pl.semaphore_signal(near_sems.at[1], inc=1, **at(sibling, me))
    for i in range(7):
        pltpu.make_async_remote_copy(
            src_ref=aux_all.at[here], dst_ref=aux_all.at[here],
            send_sem=p_sem.at[0], recv_sem=p_sem.at[1], **at(cut, near(i)[3])
        ).start()
    pl.semaphore_wait(near_sems.at[1], 1)
    for i in range(3):
        pl.semaphore_signal(near_sems.at[2], inc=1, **at(chip_at(i), me))

    loads[3].wait()
    loads[4].wait()
    loads[5].wait()

    @pl.when(working)
    def _():
        row_at = jnp.where(core == 0, pos[0, 0], pos[1, 0])
        col_at = jnp.where(core == 0, pos[0, 1], pos[1, 1])
        wave[...] = rolled_probe(probe, row_at, col_at)

    pltpu.make_async_copy(aux_all.at[0:7], aux_all.at[0:7], p_sem.at[1]).wait()
    pl.semaphore_wait(near_sems.at[2], 3)
    pltpu.make_async_copy(cells.at[0:11], cells.at[0:11], a_sem.at[1]).wait()

    blocks = [cells[n].astype(F32) for n in range(12)]
    for third in range(3):
        for h in range(2):
            for c in range(3):
                for plane in range(2):
                    first = 8 * c + 4 * plane
                    rows = [blocks[4 * third + 2 * h + k][first : first + 4] for k in range(2)]
                    strips[third, h, c, plane] = jnp.concatenate(rows, 0)

    row_here = 32 * (sub >> 2) + (sub & 3) + row_base

    def masks(p, j):
        a = aux_all[p, 2 * j : 2 * j + 1, :]
        b = aux_all[p, 2 * j + 1 : 2 * j + 2, :]
        in_row = [[((row_here + (WIN * third + 64 * h) - a) & -WIN) == 0 for third in range(3)] for h in range(2)]
        in_col = [((lane + WIN * c - b) & -WIN) == 0 for c in range(3)]
        return in_row, in_col

    def pick(p):
        for j in range(2):
            in_row, in_col = masks(p, j)
            tiles = []
            for plane in range(2):
                for h in range(2):
                    cand = []
                    for third in range(3):
                        c0, c1, c2 = (strips[third, h, c, plane] for c in range(3))
                        cand.append(jnp.where(in_col[0], c0, jnp.where(in_col[1], c1, c2)))
                    tiles.append(jnp.where(in_row[h][0], cand[0], jnp.where(in_row[h][1], cand[1], cand[2])))
            pieces[2 * p + j] = jnp.concatenate(tiles, 0).astype(BF16)

    def piece_send(yi, zi, j, to):
        pltpu.make_async_remote_copy(
            src_ref=pieces.at[2 * (4 * yi + zi) + j], dst_ref=win.at[cut, q],
            send_sem=b_send, recv_sem=b_recv.at[cut], **at(2 * worker(yi, zi, j) + j, to)
        ).start()

    def pick_and_send(i, carry):
        yi, zi, _, to = near(i)
        pick(4 * yi + zi)
        for j in range(2):
            pl.when(worker(yi, zi, j) != x)(functools.partial(piece_send, yi, zi, j, to))
        return carry

    def send_here(i, carry):
        yi, zi, _, to = near(i)
        for j in range(2):
            pl.when(worker(yi, zi, j) == x)(functools.partial(piece_send, yi, zi, j, to))
        return carry

    lax.fori_loop(0, 7, pick_and_send, 0)
    lax.fori_loop(0, 7, send_here, 0)
    pick(here)
    piece_send(y_in, z_in, 1 - core, me)

    @pl.when(working)
    def _():
        pltpu.make_async_copy(pieces.at[2 * here + core], win.at[cut, q], b_recv.at[cut]).start()

    @pl.when(jnp.logical_not(working))
    def _():
        piece_send(y_in, z_in, core, me)

    def window(s):
        w = win[s].astype(F32)
        return jnp.concatenate([w[:, 0:16].reshape(WIN, WIN), w[:, 16:32].reshape(WIN, WIN)], 1)

    def pair(i):
        return (tab[i, 0], tab[i, 1])

    def arrive(s):
        pltpu.make_async_copy(win.at[s], win.at[s], b_recv.at[s]).wait()
        psi = wave[...]
        psis[s] = psi
        return complex_mul(psi, window(s))

    def forward(s, carry):
        wave[...] = sandwich(arrive(s), pair(0), pair(1))
        return carry

    def residual(last):
        far_field = sandwich(last, pair(2), pair(3))
        far_re, far_im = far_field[:, :WIN], far_field[:, WIN:]
        live = jnp.where(core < counts[0], 1.0, 0.0).astype(F32)
        excess = (far_re * far_re + far_im * far_im - inten[...]) * live
        wave[...] = sandwich(jnp.concatenate([excess * far_re, -(excess * far_im)], 1), pair(2), pair(4))

    def send_gradient(s, u):
        g = complex_mul(psis[s], u)
        both, steps = pack(g[:, :WIN].reshape(8, 16, WIN), -g[:, WIN:].reshape(8, 16, WIN), 4)
        steps = jnp.broadcast_to(steps[:, None], (4, 2, 1, WIN)).reshape(8, 1, WIN)
        esend[pl.ds(8 * s, 8)] = jnp.concatenate([both, steps], 1)
        for i in range(7):
            send_one(s, *near(i)[2:])

    def send_one(s, q_to, to):
        pltpu.make_async_remote_copy(
            src_ref=esend.at[8 * s + q_to], dst_ref=erecv.at[core, here],
            send_sem=e_send, recv_sem=e_recv, **at(s, to)
        ).start()

    def send_own(s):
        @pl.when(s != cut)
        def _():
            send_one(s, q, me)

        @pl.when(s == cut)
        def _():
            pltpu.make_async_copy(esend.at[8 * s + q], erecv.at[core, here], e_recv).start()

    def backward(n, carry):
        s = 7 - n
        u = wave[...]
        send_gradient(s, u)
        wave[...] = sandwich(complex_mul(u, window(s)), pair(0), pair(1))
        send_own(s)
        return carry

    @pl.when(working)
    def _():
        lax.fori_loop(0, 7, forward, 0)
        residual(arrive(7))
        lax.fori_loop(0, 7, backward, 0)
        send_gradient(0, wave[...])
        send_own(0)

    pltpu.make_async_copy(erecv, erecv, e_recv).wait()

    def place(h, p, sums):
        sums = list(sums)
        for j in range(2):
            in_row, in_col = masks(p, j)
            vals = unpack(erecv[j, p, 8 * h : 8 * h + 8, :], erecv[j, p, 16:17, :], 1.0)
            for plane in range(2):
                for third in range(3):
                    kept = jnp.where(in_row[h][third], vals[plane], 0.0)
                    for c in range(3):
                        i = (third * 3 + c) * 2 + plane
                        sums[i] = sums[i] + jnp.where(in_col[c], kept, 0.0)
        return tuple(sums)

    def send_sum(n_to):
        pltpu.make_async_remote_copy(
            src_ref=fsend.at[n_to], dst_ref=frecv.at[n_mine], send_sem=f_sem.at[0], recv_sem=f_sem.at[1],
            **at(cut, 8 * n_to + 4 * bit_b + z_in)
        ).start()

    for h in range(2):
        sums = tuple(jnp.zeros((8, WIN), F32) for _ in range(18))
        sums = lax.fori_loop(0, 8, functools.partial(place, h), sums)
        for third in range(3):
            re, im = (jnp.stack([sums[(third * 3 + c) * 2 + plane] for c in range(3)]) for plane in range(2))
            both, steps = pack(re, im, 1)
            for k in range(2):
                rows = [both[c, 4 * k : 4 * k + 4] for c in range(3)] + [steps[0]]
                fsend[4 * third + 2 * h + k] = jnp.concatenate(rows, 0)
        for third in range(3):
            for k in range(2):
                n_to = 4 * third + 2 * h + k
                pl.when(n_to != n_mine)(functools.partial(send_sum, n_to))
    frecv[n_mine] = fsend[n_mine]

    @pl.when(working)
    def _():
        pltpu.make_async_copy(pieces.at[0:15], pieces.at[0:15], b_send).wait()
        pltpu.make_async_copy(esend.at[0:63], esend.at[0:63], e_send).wait()

    @pl.when(jnp.logical_not(working))
    def _():
        pltpu.make_async_copy(pieces, pieces, b_send).wait()

    for ref, sem in (
        (cells.at[0:11], a_sem.at[0]),
        (aux_all.at[0:7], p_sem.at[0]),
        (fsend.at[0:11], f_sem.at[0]),
        (frecv.at[0:11], f_sem.at[1]),
    ):
        pltpu.make_async_copy(ref, ref, sem).wait()
    total = [jnp.zeros((12, WIN), F32)] * 2
    for n in range(12):
        part = unpack(frecv[n, 0:12, :], frecv[n, 12:13, :], GRAD_SCALE)
        total = [total[plane] + part[plane] for plane in range(2)]
    for rr in range(4):
        for c in range(3):
            first = (3 * rr + c) * WIN
            both = [total[plane][4 * c + rr : 4 * c + rr + 1] for plane in range(2)]
            out_ref[:, first : first + WIN] = jnp.concatenate(both, 0)


def body(tab, object_slices, probe_wave, intensity, positions, counts):
    hbm = pl.BlockSpec(memory_space=pltpu.HBM)
    vmem = pl.BlockSpec(memory_space=pltpu.VMEM)
    dma = pltpu.SemaphoreType.DMA
    out = pl.pallas_call(
        kernel,
        out_shape=pltpu.VMEM((2, 12 * WIN), F32),
        in_specs=[hbm] * 6,
        out_specs=vmem,
        scratch_shapes=[
            pltpu.VMEM((2, 12 * WIN), BF16),
            pltpu.VMEM((32, WIN), BF16),
            pltpu.SMEM((2, 2), jnp.int32),
            pltpu.SMEM((1,), jnp.int32),
            pltpu.VMEM((2, WIN, WIN), F32),
            pltpu.VMEM((WIN, WIN), F32),
            pltpu.VMEM((5, 2, 2 * WIN, 2 * WIN), BF16),
            pltpu.VMEM((12, 32, WIN), BF16),
            pltpu.VMEM((3, 2, 3, 2, 8, WIN), F32),
            pltpu.VMEM((8, 4, WIN), jnp.int32),
            pltpu.VMEM((16, 32, WIN), BF16),
            pltpu.VMEM((8, 8, 32, WIN), BF16),
            pltpu.VMEM((8, WIN, 2 * WIN), F32),
            pltpu.VMEM((WIN, 2 * WIN), F32),
            pltpu.VMEM((64, 17, WIN), jnp.int32),
            pltpu.VMEM((2, 8, 17, WIN), jnp.int32),
            pltpu.VMEM((12, 13, WIN), jnp.int32),
            pltpu.VMEM((12, 13, WIN), jnp.int32),
            dma((6,)),
            pltpu.SemaphoreType.REGULAR((3,)),
            dma((2,)), dma((2,)),
            dma, dma((8,)),
            dma, dma,
            dma((2,)),
        ],
        compiler_params=pltpu.CompilerParams(
            collective_id=0, has_side_effects=True, vmem_limit_bytes=60 << 20
        ),
    )(object_slices, positions, counts, probe_wave, intensity, tab)
    return out.reshape(1, 2, 12 * WIN)


def solution(mesh):
    tab = tables()
    in_specs = (P("cuts", None, "scan"), P(), P("scan", None, None), P("scan", None), P("scan"))
    out_specs = P("cuts", None, "scan")
    return jax.shard_map(
        functools.partial(body, tab), mesh=mesh, in_specs=in_specs, out_specs=out_specs, check_vma=False
    )
```

```python
import functools

import jax
import jax.numpy as jnp
import ml_dtypes
import numpy as np
from jax import lax
from jax.experimental import pallas as pl
from jax.experimental.pallas import tpu as pltpu
from jax.sharding import PartitionSpec as P

WIN = 128
FRESNEL = 0.5
GRAD_SCALE = 0.25
NZ = 12
FARTHEST = (5, 7, 4, 8, 2, 10, 1, 11, 6, 3, 9)
F32 = jnp.float32
BF16 = jnp.bfloat16
MESH = pl.DeviceIdType.MESH


def row_order():
    rho = np.arange(WIN)
    q, h, k, rr = rho // 16, (rho // 8) % 2, (rho // 4) % 2, rho % 4
    return 64 * h + 32 * k + 16 * (q // 4) + 4 * (q % 4) + rr


def split_table(mat):
    hi = mat.astype(ml_dtypes.bfloat16)
    lo = (mat - hi.astype(np.float64)).astype(ml_dtypes.bfloat16)
    return np.stack([hi, lo])


def tables():
    k = np.arange(WIN)
    four = np.exp(-2j * np.pi * ((k[:, None] * k[None, :]) % WIN) / WIN) / np.sqrt(WIN)
    freq = np.where(k < WIN // 2, k, k - WIN).astype(np.float64)
    half = np.exp(-1j * np.pi * FRESNEL * freq * freq / WIN)
    kern = np.conj(four.T) @ (half[:, None] * four)
    order = row_order()

    def right(mat):
        return split_table(np.block([[mat.real, mat.imag], [-mat.imag, mat.real]]))

    def left(mat):
        return split_table(np.block([[mat.real, -mat.imag], [mat.imag, mat.real]]))

    return np.stack(
        [
            right(kern),
            left(kern[order][:, order]),
            right(four),
            left(four[:, order]),
            left(four[order]),
        ]
    )


def dot(a, b):
    return jnp.dot(a, b, preferred_element_type=F32)


def split(x):
    hi = x.astype(BF16)
    return hi, (x - hi.astype(F32)).astype(BF16)


def sandwich(x, right, left):
    hi, lo = split(x)
    both = dot(jnp.concatenate([hi, lo], 0), right[0])
    mid = both[:WIN] + both[WIN:] + dot(hi, right[1])
    mid = jnp.concatenate([mid[:, :WIN], mid[:, WIN:]], 0)
    hi, lo = split(mid)
    both = dot(left[0], jnp.concatenate([hi, lo], 1))
    out = both[:, :WIN] + both[:, WIN:] + dot(left[1], hi)
    return jnp.concatenate([out[:WIN], out[WIN:]], 1)


def complex_mul(x, w):
    x_re, x_im, w_re, w_im = x[:, :WIN], x[:, WIN:], w[:, :WIN], w[:, WIN:]
    return jnp.concatenate([x_re * w_re - x_im * w_im, x_re * w_im + x_im * w_re], 1)


def rolled_probe(probe_ref, row_at, col_at):
    shape = (WIN, WIN)
    rho = lax.broadcasted_iota(jnp.int32, shape, 0)
    lane = lax.broadcasted_iota(jnp.int32, shape, 1)
    t = (
        64 * ((rho >> 3) & 1)
        + 32 * ((rho >> 2) & 1)
        + 16 * ((rho >> 6) & 1)
        + 4 * ((rho >> 4) & 3)
        + (rho & 3)
    )
    rows = (((t - lane - row_at) & (WIN - 1)) == 0).astype(F32).astype(BF16)
    cols = (((lane - rho - col_at) & (WIN - 1)) == 0).astype(F32).astype(BF16)
    halves = []
    for plane in range(2):
        rest = probe_ref[plane]
        total = jnp.zeros(shape, F32)
        for _ in range(3):
            part = rest.astype(BF16)
            rest = rest - part.astype(F32)
            total = total + dot(dot(rows, part).astype(BF16), cols)
        halves.append(total)
    return jnp.concatenate(halves, 1)


STEPS = 256
TOP = 32760.0


def scale_of(steps):
    return jnp.exp(steps.astype(F32) * (np.log(2.0) / STEPS))


def pack(re, im, groups):
    def grouped(part):
        return part.reshape(groups, -1, 8, WIN)

    most = jnp.max(grouped(jnp.maximum(jnp.abs(re), jnp.abs(im))), axis=1)
    most = jnp.max(most, axis=1, keepdims=True)
    steps = jnp.ceil(jnp.log(jnp.maximum(most, 1e-30)) * (STEPS / np.log(2.0))).astype(jnp.int32)
    factor = (TOP * scale_of(-steps))[:, None]
    whole_re, whole_im = (jnp.floor(grouped(part) * factor + 0.5).astype(jnp.int32) for part in (re, im))
    return ((whole_re << 16) | (whole_im & 0xFFFF)).reshape(re.shape), steps


def unpack(both, steps, factor):
    scale = scale_of(steps) * (factor / TOP)
    return (both >> 16).astype(F32) * scale, ((both << 16) >> 16).astype(F32) * scale


def rem(a, b):
    return lax.rem(a, jnp.int32(b))


def div(a, b):
    return lax.div(a, jnp.int32(b))


def kernel(
    obj_ref, pos_ref, counts_ref, probe_ref, inten_ref, tab_ref,
    out_ref,
    raw, obj, pos, counts, probe, inten, tab,
    cells, strips, aux_all, pieces, win, psis, wave, esend, erecv, fsend, frecv,
    in_sems, near_sems, a_sem, p_sem, b_send, b_recv, e_send, e_recv, f_sem,
):
    cut = lax.axis_index("cuts")
    me = lax.axis_index("scan")
    x, core = div(cut, 2), rem(cut, 2)
    y, z = div(me, NZ), rem(me, NZ)
    z_block, z_in = div(z, 4), rem(z, 4)
    y_block, y_in = div(y, 2), rem(y, 2)
    bit_b = rem(y_in + z_block, 2)
    q = 4 * bit_b + z_in
    n_mine = div(me, 8)
    row_base = 16 * bit_b + 4 * z_in

    def worker(yi, zi, j):
        return rem(yi + zi + j, 2)

    working = x == worker(y_in, z_in, core)

    def far(d):
        n = rem(n_mine + d, 12)
        return n, 8 * n + 4 * bit_b + z_in

    def mate(dy, dz):
        yi, zi = rem(y_in + dy, 2), rem(z_in + dz, 4)
        return yi, zi, 4 * rem(yi + z_block, 2) + zi, (2 * y_block + yi) * NZ + 4 * z_block + zi

    def near(i):
        flag = lambda hit: jnp.asarray(hit).astype(jnp.int32)
        i = jnp.asarray(i, jnp.int32)
        other_row, same_column = flag(i < 3) + flag(i == 6), flag(i == 6)
        up = rem(i, 3)
        down = 3 - up
        upper = flag(z_in >= 2)
        column = upper * (up + flag(up >= z_in)) + (1 - upper) * (down - flag(down <= z_in))
        zi = same_column * z_in + (1 - same_column) * column
        yi = other_row * (1 - y_in) + (1 - other_row) * y_in
        return yi, zi, 4 * rem(yi + z_block, 2) + zi, (2 * y_block + yi) * NZ + 4 * z_block + zi

    def at(cut_to, scan_to):
        return dict(device_id={"cuts": cut_to, "scan": scan_to}, device_id_type=MESH)

    sibling = cut + 1 - 2 * core

    def chip_at(i):
        x_to = i + (x <= i).astype(jnp.int32)
        return 2 * x_to + core

    loads = [
        (obj_ref.at[0], raw), (pos_ref, pos), (counts_ref, counts), (probe_ref, probe), (inten_ref.at[core], inten), (tab_ref, tab),
    ]
    loads = [pltpu.make_async_copy(src, dst, in_sems.at[i]) for i, (src, dst) in enumerate(loads)]
    for load in loads:
        load.start()

    barrier = pltpu.get_barrier_semaphore()
    for d in FARTHEST:
        pl.semaphore_signal(barrier, inc=1, **at(cut, far(d)[1]))
    for d in range(1, 4):
        pl.semaphore_signal(barrier, inc=1, **at(cut, mate(0, d)[3]))
    pl.semaphore_signal(barrier, inc=1, **at(cut, mate(1, 0)[3]))
    pl.semaphore_signal(barrier, inc=1, **at(sibling, me))
    for i in range(3):
        pl.semaphore_signal(barrier, inc=1, **at(chip_at(i), me))

    loads[0].wait()
    flat_obj = raw[...].astype(F32)
    rows = []
    for c in range(3):
        for plane in range(2):
            for rr in range(4):
                first = (3 * rr + c) * WIN
                rows.append(flat_obj[plane : plane + 1, first : first + WIN])
    obj[...] = jnp.concatenate(rows + [jnp.zeros((8, WIN), F32)], 0).astype(BF16)
    pl.semaphore_wait(barrier, 19)

    pl.semaphore_signal(near_sems.at[0], inc=1, **at(cut, mate(1, 0)[3]))

    for d in FARTHEST:
        pltpu.make_async_remote_copy(
            src_ref=obj, dst_ref=cells.at[n_mine], send_sem=a_sem.at[0], recv_sem=a_sem.at[1], **at(cut, far(d)[1])
        ).start()
    cells[n_mine] = obj[...]

    loads[1].wait()
    loads[2].wait()
    here = 4 * y_in + z_in
    sub = lax.broadcasted_iota(jnp.int32, (8, WIN), 0)
    lane = lax.broadcasted_iota(jnp.int32, (8, WIN), 1)
    mine = jnp.where(
        sub == 0, pos[0, 0], jnp.where(sub == 1, pos[0, 1], jnp.where(sub == 2, pos[1, 0], pos[1, 1]))
    )
    aux_all[here] = mine[0:4]
    pl.semaphore_wait(near_sems.at[0], 1)
    pl.semaphore_signal(near_sems.at[1], inc=1, **at(sibling, me))
    for i in range(7):
        pltpu.make_async_remote_copy(
            src_ref=aux_all.at[here], dst_ref=aux_all.at[here],
            send_sem=p_sem.at[0], recv_sem=p_sem.at[1], **at(cut, near(i)[3])
        ).start()
    pl.semaphore_wait(near_sems.at[1], 1)
    for i in range(3):
        pl.semaphore_signal(near_sems.at[2], inc=1, **at(chip_at(i), me))

    loads[3].wait()
    loads[4].wait()
    loads[5].wait()

    @pl.when(working)
    def _():
        row_at = jnp.where(core == 0, pos[0, 0], pos[1, 0])
        col_at = jnp.where(core == 0, pos[0, 1], pos[1, 1])
        wave[...] = rolled_probe(probe, row_at, col_at)

    pltpu.make_async_copy(aux_all.at[0:7], aux_all.at[0:7], p_sem.at[1]).wait()
    pl.semaphore_wait(near_sems.at[2], 3)
    pltpu.make_async_copy(cells.at[0:11], cells.at[0:11], a_sem.at[1]).wait()

    blocks = [cells[n].astype(F32) for n in range(12)]
    for third in range(3):
        for h in range(2):
            for c in range(3):
                for plane in range(2):
                    first = 8 * c + 4 * plane
                    rows = [blocks[4 * third + 2 * h + k][first : first + 4] for k in range(2)]
                    strips[third, h, c, plane] = jnp.concatenate(rows, 0)

    row_here = 32 * (sub >> 2) + (sub & 3) + row_base

    def masks(p, j):
        a = aux_all[p, 2 * j : 2 * j + 1, :]
        b = aux_all[p, 2 * j + 1 : 2 * j + 2, :]
        in_row = [[((row_here + (WIN * third + 64 * h) - a) & -WIN) == 0 for third in range(3)] for h in range(2)]
        in_col = [((lane + WIN * c - b) & -WIN) == 0 for c in range(3)]
        return in_row, in_col

    def pick(p):
        for j in range(2):
            in_row, in_col = masks(p, j)
            tiles = []
            for plane in range(2):
                for h in range(2):
                    cand = []
                    for third in range(3):
                        c0, c1, c2 = (strips[third, h, c, plane] for c in range(3))
                        cand.append(jnp.where(in_col[0], c0, jnp.where(in_col[1], c1, c2)))
                    tiles.append(jnp.where(in_row[h][0], cand[0], jnp.where(in_row[h][1], cand[1], cand[2])))
            pieces[2 * p + j] = jnp.concatenate(tiles, 0).astype(BF16)

    def piece_send(yi, zi, j, to):
        pltpu.make_async_remote_copy(
            src_ref=pieces.at[2 * (4 * yi + zi) + j], dst_ref=win.at[cut, q],
            send_sem=b_send, recv_sem=b_recv.at[cut], **at(2 * worker(yi, zi, j) + j, to)
        ).start()

    def pick_and_send(i, carry):
        yi, zi, _, to = near(i)
        pick(4 * yi + zi)
        for j in range(2):
            pl.when(worker(yi, zi, j) != x)(functools.partial(piece_send, yi, zi, j, to))
        return carry

    def send_here(i, carry):
        yi, zi, _, to = near(i)
        for j in range(2):
            pl.when(worker(yi, zi, j) == x)(functools.partial(piece_send, yi, zi, j, to))
        return carry

    lax.fori_loop(0, 7, pick_and_send, 0)
    lax.fori_loop(0, 7, send_here, 0)
    pick(here)
    piece_send(y_in, z_in, 1 - core, me)

    @pl.when(working)
    def _():
        pltpu.make_async_copy(pieces.at[2 * here + core], win.at[cut, q], b_recv.at[cut]).start()

    @pl.when(jnp.logical_not(working))
    def _():
        piece_send(y_in, z_in, core, me)

    def window(s):
        w = win[s].astype(F32)
        return jnp.concatenate([w[:, 0:16].reshape(WIN, WIN), w[:, 16:32].reshape(WIN, WIN)], 1)

    def pair(i):
        return (tab[i, 0], tab[i, 1])

    def arrive(s):
        pltpu.make_async_copy(win.at[s], win.at[s], b_recv.at[s]).wait()
        psi = wave[...]
        psis[s] = psi
        return complex_mul(psi, window(s))

    def forward(s, carry):
        wave[...] = sandwich(arrive(s), pair(0), pair(1))
        return carry

    def residual(last):
        far_field = sandwich(last, pair(2), pair(3))
        far_re, far_im = far_field[:, :WIN], far_field[:, WIN:]
        live = jnp.where(core < counts[0], 1.0, 0.0).astype(F32)
        excess = (far_re * far_re + far_im * far_im - inten[...]) * live
        wave[...] = sandwich(jnp.concatenate([excess * far_re, -(excess * far_im)], 1), pair(2), pair(4))

    def send_gradient(s, u):
        g = complex_mul(psis[s], u)
        both, steps = pack(g[:, :WIN].reshape(8, 16, WIN), -g[:, WIN:].reshape(8, 16, WIN), 4)
        steps = jnp.broadcast_to(steps[:, None], (4, 2, 1, WIN)).reshape(8, 1, WIN)
        esend[pl.ds(8 * s, 8)] = jnp.concatenate([both, steps], 1)
        for i in range(7):
            send_one(s, *near(i)[2:])

    def send_one(s, q_to, to):
        pltpu.make_async_remote_copy(
            src_ref=esend.at[8 * s + q_to], dst_ref=erecv.at[core, here],
            send_sem=e_send, recv_sem=e_recv, **at(s, to)
        ).start()

    def send_own(s):
        @pl.when(s != cut)
        def _():
            send_one(s, q, me)

        @pl.when(s == cut)
        def _():
            pltpu.make_async_copy(esend.at[8 * s + q], erecv.at[core, here], e_recv).start()

    def backward(n, carry):
        s = 7 - n
        u = wave[...]
        send_gradient(s, u)
        wave[...] = sandwich(complex_mul(u, window(s)), pair(0), pair(1))
        send_own(s)
        return carry

    @pl.when(working)
    def _():
        lax.fori_loop(0, 7, forward, 0)
        residual(arrive(7))
        lax.fori_loop(0, 7, backward, 0)
        send_gradient(0, wave[...])
        send_own(0)

    pltpu.make_async_copy(erecv, erecv, e_recv).wait()

    def place(h, p, sums):
        sums = list(sums)
        for j in range(2):
            in_row, in_col = masks(p, j)
            vals = unpack(erecv[j, p, 8 * h : 8 * h + 8, :], erecv[j, p, 16:17, :], 1.0)
            for plane in range(2):
                for third in range(3):
                    kept = jnp.where(in_row[h][third], vals[plane], 0.0)
                    for c in range(3):
                        i = (third * 3 + c) * 2 + plane
                        sums[i] = sums[i] + jnp.where(in_col[c], kept, 0.0)
        return tuple(sums)

    def send_sum(n_to):
        pltpu.make_async_remote_copy(
            src_ref=fsend.at[n_to], dst_ref=frecv.at[n_mine], send_sem=f_sem.at[0], recv_sem=f_sem.at[1],
            **at(cut, 8 * n_to + 4 * bit_b + z_in)
        ).start()

    for h in range(2):
        sums = tuple(jnp.zeros((8, WIN), F32) for _ in range(18))
        sums = lax.fori_loop(0, 8, functools.partial(place, h), sums, unroll=2)
        for third in range(3):
            re, im = (jnp.stack([sums[(third * 3 + c) * 2 + plane] for c in range(3)]) for plane in range(2))
            both, steps = pack(re, im, 1)
            for k in range(2):
                rows = [both[c, 4 * k : 4 * k + 4] for c in range(3)] + [steps[0]]
                fsend[4 * third + 2 * h + k] = jnp.concatenate(rows, 0)
        for third in range(3):
            for k in range(2):
                n_to = 4 * third + 2 * h + k
                pl.when(n_to != n_mine)(functools.partial(send_sum, n_to))
    frecv[n_mine] = fsend[n_mine]

    @pl.when(working)
    def _():
        pltpu.make_async_copy(pieces.at[0:15], pieces.at[0:15], b_send).wait()
        pltpu.make_async_copy(esend.at[0:63], esend.at[0:63], e_send).wait()

    @pl.when(jnp.logical_not(working))
    def _():
        pltpu.make_async_copy(pieces, pieces, b_send).wait()

    for ref, sem in (
        (cells.at[0:11], a_sem.at[0]),
        (aux_all.at[0:7], p_sem.at[0]),
        (fsend.at[0:11], f_sem.at[0]),
        (frecv.at[0:11], f_sem.at[1]),
    ):
        pltpu.make_async_copy(ref, ref, sem).wait()
    total = [jnp.zeros((12, WIN), F32)] * 2
    for n in range(12):
        part = unpack(frecv[n, 0:12, :], frecv[n, 12:13, :], GRAD_SCALE)
        total = [total[plane] + part[plane] for plane in range(2)]
    for rr in range(4):
        for c in range(3):
            first = (3 * rr + c) * WIN
            both = [total[plane][4 * c + rr : 4 * c + rr + 1] for plane in range(2)]
            out_ref[:, first : first + WIN] = jnp.concatenate(both, 0)


def body(tab, object_slices, probe_wave, intensity, positions, counts):
    hbm = pl.BlockSpec(memory_space=pltpu.HBM)
    vmem = pl.BlockSpec(memory_space=pltpu.VMEM)
    dma = pltpu.SemaphoreType.DMA
    out = pl.pallas_call(
        kernel,
        out_shape=pltpu.VMEM((2, 12 * WIN), F32),
        in_specs=[hbm] * 6,
        out_specs=vmem,
        scratch_shapes=[
            pltpu.VMEM((2, 12 * WIN), BF16),
            pltpu.VMEM((32, WIN), BF16),
            pltpu.SMEM((2, 2), jnp.int32),
            pltpu.SMEM((1,), jnp.int32),
            pltpu.VMEM((2, WIN, WIN), F32),
            pltpu.VMEM((WIN, WIN), F32),
            pltpu.VMEM((5, 2, 2 * WIN, 2 * WIN), BF16),
            pltpu.VMEM((12, 32, WIN), BF16),
            pltpu.VMEM((3, 2, 3, 2, 8, WIN), F32),
            pltpu.VMEM((8, 4, WIN), jnp.int32),
            pltpu.VMEM((16, 32, WIN), BF16),
            pltpu.VMEM((8, 8, 32, WIN), BF16),
            pltpu.VMEM((8, WIN, 2 * WIN), F32),
            pltpu.VMEM((WIN, 2 * WIN), F32),
            pltpu.VMEM((64, 17, WIN), jnp.int32),
            pltpu.VMEM((2, 8, 17, WIN), jnp.int32),
            pltpu.VMEM((12, 13, WIN), jnp.int32),
            pltpu.VMEM((12, 13, WIN), jnp.int32),
            dma((6,)),
            pltpu.SemaphoreType.REGULAR((3,)),
            dma((2,)), dma((2,)),
            dma, dma((8,)),
            dma, dma,
            dma((2,)),
        ],
        compiler_params=pltpu.CompilerParams(
            collective_id=0, has_side_effects=True, vmem_limit_bytes=60 << 20
        ),
    )(object_slices, positions, counts, probe_wave, intensity, tab)
    return out.reshape(1, 2, 12 * WIN)


def solution(mesh):
    tab = tables()
    in_specs = (P("cuts", None, "scan"), P(), P("scan", None, None), P("scan", None), P("scan"))
    out_specs = P("cuts", None, "scan")
    return jax.shard_map(
        functools.partial(body, tab), mesh=mesh, in_specs=in_specs, out_specs=out_specs, check_vma=False
    )
```
